32 devices in a mesh: seq: 8 (over z, y), chan: 4 (over x, core).
Axes of the slice: x: 2, y: 2, z: 4, core: 2. Of those that a mesh axis runs over, the one named last changes fastest.
Arguments:
- query_in: bfloat16 [1024, 6144], P('seq', 'chan'), may hold values from -6 to 6
- key_in: bfloat16 [1024, 6144], P('seq', 'chan'), may hold values from -6 to 6
- value_in: bfloat16 [1024, 6144], P('seq', 'chan'), may hold values from -6 to 6
- filters: bfloat16 [384, 128], P('chan'), may hold values from -0.5 to 0.5
- doc_lengths: int32 [16], replicated, may hold values from 1 to 256, 1024 in all
- w_out: bfloat16 [6144, 6144], P('chan'), may hold values from -0.109375 to 0.109375
- cotangent: bfloat16 [1024, 6144], P('seq', 'chan'), may hold values from -6 to 6
Outputs:
- block_out: bfloat16 [1024, 6144], P('seq', 'chan')
- grad_query: bfloat16 [1024, 6144], P('seq', 'chan')
- grad_key: bfloat16 [1024, 6144], P('seq', 'chan')
- grad_value: bfloat16 [1024, 6144], P('seq', 'chan')
- grad_w_out: bfloat16 [6144, 6144], P('chan', 'seq')
- grad_filters: float32 [384, 128], P('chan', 'seq')
The draws below stay inside these ranges and needn't reach their ends.
Inputs may be any that keep to these rules, and one draw needn't show every extreme that they name: `doc_lengths`: the lengths sum to 1024.
All inputs are finite; a program needn't handle non-finite values.
Results may differ from the reference program's by a relative error of at most 0.02.
Values may be sent and summed in bfloat16 or wider, within the bound.
A program may use at most 128 MiB of HBM per device.

```python
import math
import jax
import jax.numpy as jnp
import numpy as np
from jax import lax

D = 6144
GROUP = 16
LTAP = 128
NDOCS = 16
TOK_DEV = 128
TOKENS = 1024
CH_DEV = 1536
NGROUPS = 384
N_SEQ = 8
N_CHAN = 4


def strengthened(drawn, key, source, target, parts, factor):
    owner, partner = [(jnp.arange(drawn.shape[position]) // (drawn.shape[position] // parts)).reshape([-1 if axis == position else 1 for axis in range(drawn.ndim)]) for position in (source, target)]
    chosen = jax.random.permutation(key, parts)[partner]
    strong = (owner == chosen) | (owner == (partner + parts // 2) % parts)
    return jnp.where(strong, factor * drawn, drawn)


def steps_of(key, extent, shards, low, largest):
    def one(position, blocks):
        draws = jax.random.uniform(jax.random.fold_in(jax.random.fold_in(key, 6), position), (blocks,), jnp.float32, low / len(shards), largest / len(shards))
        return jnp.repeat(jnp.exp(draws), extent[position] // blocks).reshape((-1,) + (1,) * (len(extent) - position - 1))

    loudness = one(*shards[0])
    for cut in shards[1:]:
        loudness = loudness * one(*cut)
    return loudness


def length_profile(amount, total, most, lean):
    weights = [(1 << 20) // math.isqrt(rank ** lean) + 1 for rank in range(2, amount + 1)]
    surplus, given = total - most - (amount - 1), [1] * (amount - 1)
    while surplus > 0:
        free = [i for i in range(amount - 1) if given[i] < most]
        mass, remaining = sum([weights[i] for i in free]), surplus
        for i in free:
            addition = min(most - given[i], max(1, remaining * weights[i] // mass), surplus)
            given[i] = given[i] + addition
            surplus = surplus - addition
    return np.array([most] + given)


def ragged_sizes(own_key, number_of, total, limit, slope):
    if number_of == 2:
        one = jax.random.randint(own_key, (), max(1, total - limit), min(limit, total - 1) + 1)
        return jnp.stack([one, total - one])
    tallies = jnp.asarray(length_profile(number_of, total, limit, slope), jnp.int32)
    pairs = (number_of - 1) // 2
    source_of, receiver = tallies[1:1 + 2 * pairs:2], tallies[2:2 + 2 * pairs:2]
    room = jnp.minimum(source_of - 1, limit - receiver)
    moved = jax.random.randint(jax.random.fold_in(own_key, 1), (pairs,), 0, 1 << 20) % (room + 1)
    tallies = tallies.at[1:1 + 2 * pairs:2].set(source_of - moved).at[2:2 + 2 * pairs:2].set(receiver + moved)
    return tallies[jax.random.permutation(jax.random.fold_in(own_key, 2), number_of)]


def bell_draw(stream_key, dims, deviation, reach, pieces=(), kind=jnp.bfloat16):
    gain = steps_of(stream_key, dims, pieces, -0.22, 0.18) if pieces else 1.0
    values = jax.random.normal(stream_key, dims, jnp.float32) * deviation * gain
    return jnp.minimum(jnp.maximum(values, -reach), reach).astype(kind)


def gaussian_with(rng, extent, spread, bound, pieces, heavy, kind=jnp.bfloat16):
    entries = spread * jax.random.normal(rng, extent, jnp.float32)
    if pieces:
        entries = entries * steps_of(rng, extent, pieces, -0.22, 0.18)
    return jnp.clip(strengthened(entries, jax.random.fold_in(rng, 3), *heavy), -bound, bound).astype(kind)


def setup_inputs(seed: int = 0) -> dict:
    key_list = jax.random.split(jax.random.key(seed), 8)
    query_in = bell_draw(key_list[0], (TOKENS, D), 1.0, 6.0, ((0, 8), (1, 4)))
    key_in = bell_draw(key_list[1], (TOKENS, D), 1.0, 6.0, ((0, 8), (1, 4)))
    value_in = bell_draw(key_list[2], (TOKENS, D), 1.0, 6.0, ((0, 8), (1, 4)))
    filters = bell_draw(key_list[3], (NGROUPS, LTAP), LTAP ** -0.5, 0.5, ((0, 4),))
    doc_lengths = ragged_sizes(key_list[4], NDOCS, TOKENS, TOKENS // 4, 2).astype(jnp.int32)
    w_out = gaussian_with(key_list[5], (D, D), D ** -0.5, 0.109375, ((0, 4),), (0, 1, 4, 2.0))
    cotangent = gaussian_with(key_list[6], (TOKENS, D), 1.0, 6.0, ((0, 8), (1, 4)), (0, 1, 8, 2.0))
    return dict(query_in=query_in, key_in=key_in, value_in=value_in, filters=filters, doc_lengths=doc_lengths, w_out=w_out, cotangent=cotangent)


def doc_start(positions, starts):
    before = starts[None, :] <= positions[:, None]
    return lax.optimization_barrier(jnp.max(jnp.where(before, starts[None, :], 0), axis=1))

def reference(query_in, key_in, value_in, filters, doc_lengths, w_out, cotangent):
    starts = jnp.cumsum(doc_lengths) - doc_lengths
    positions = jnp.arange(TOKENS, dtype=jnp.int32)
    own_start = doc_start(positions, starts)
    tap_reach = LTAP - 1
    product_kv = lax.optimization_barrier((key_in.astype(jnp.float32) * value_in.astype(jnp.float32)).astype(jnp.bfloat16)).astype(jnp.float32)
    per_channel = jnp.repeat(filters.astype(jnp.float32), GROUP, axis=0)
    mixed_pad = jnp.concatenate([jnp.zeros((tap_reach, D), jnp.float32), product_kv], axis=0)
    tap_ids = jnp.arange(LTAP, dtype=jnp.int32)

    def forward_tap(running, tap):
        source = lax.dynamic_slice_in_dim(mixed_pad, tap_reach - tap, TOKENS, 0)
        keep = (positions - tap >= own_start).astype(jnp.float32)
        weight_col = lax.dynamic_index_in_dim(per_channel, tap, 1, keepdims=False)
        return (running + source * keep[:, None] * weight_col[None, :], None)
    filtered, _ = lax.scan(forward_tap, jnp.zeros((TOKENS, D), jnp.float32), tap_ids)
    gated = (query_in.astype(jnp.float32) * filtered).astype(jnp.bfloat16)

    def out_group(running, index):
        rows_in = lax.dynamic_slice_in_dim(gated, index * CH_DEV, CH_DEV, 1)
        weights = lax.dynamic_slice_in_dim(w_out, index * CH_DEV, CH_DEV, 0)
        term = lax.optimization_barrier(jnp.dot(rows_in, weights, preferred_element_type=jnp.float32).astype(jnp.bfloat16))
        return (running + term.astype(jnp.float32), None)
    out_total, _ = lax.scan(out_group, jnp.zeros((TOKENS, D), jnp.float32), jnp.arange(N_CHAN, dtype=jnp.int32))
    block_out = out_total.astype(jnp.bfloat16)
    grad_in = jnp.dot(cotangent, w_out.T, preferred_element_type=jnp.float32)
    grad_gate = lax.optimization_barrier((grad_in * query_in.astype(jnp.float32)).astype(jnp.bfloat16)).astype(jnp.float32)
    grad_query = (grad_in * filtered).astype(jnp.bfloat16)
    grad_pad = jnp.concatenate([grad_gate, jnp.zeros((tap_reach, D), jnp.float32)], axis=0)

    def back_tap(running, tap):
        source = lax.dynamic_slice_in_dim(grad_pad, tap, TOKENS, 0)
        keep = (positions >= doc_start(positions + tap, starts)).astype(jnp.float32)
        weight_col = lax.dynamic_index_in_dim(per_channel, tap, 1, keepdims=False)
        return (running + source * keep[:, None] * weight_col[None, :], None)
    grad_mixed, _ = lax.scan(back_tap, jnp.zeros((TOKENS, D), jnp.float32), tap_ids)
    grad_key = (grad_mixed * value_in.astype(jnp.float32)).astype(jnp.bfloat16)
    grad_value = (grad_mixed * key_in.astype(jnp.float32)).astype(jnp.bfloat16)

    def tap_grad(running, tap):
        source = lax.dynamic_slice_in_dim(mixed_pad, tap_reach - tap, TOKENS, 0)
        keep = (positions - tap >= own_start).astype(jnp.float32)
        terms = (grad_gate * source * keep[:, None]).reshape(N_SEQ, TOK_DEV, NGROUPS, GROUP).sum(axis=(1, 3))
        shard_terms = lax.optimization_barrier(terms.astype(jnp.bfloat16)).astype(jnp.float32)
        return (running, lax.optimization_barrier(jnp.sum(shard_terms, axis=0)))
    _, per_tap = lax.scan(tap_grad, jnp.zeros((), jnp.float32), tap_ids)
    grad_filters = per_tap.T

    def weight_shard(running, index):
        rows_gated = lax.dynamic_slice_in_dim(gated, index * TOK_DEV, TOK_DEV, 0)
        rows_cot = lax.dynamic_slice_in_dim(cotangent, index * TOK_DEV, TOK_DEV, 0)
        term = lax.optimization_barrier(jnp.dot(rows_gated.T, rows_cot, preferred_element_type=jnp.float32).astype(jnp.bfloat16))
        return (running + term.astype(jnp.float32), None)
    weight_total, _ = lax.scan(weight_shard, jnp.zeros((D, D), jnp.float32), jnp.arange(N_SEQ, dtype=jnp.int32))
    grad_w_out = weight_total.astype(jnp.bfloat16)
    return (block_out, grad_query, grad_key, grad_value, grad_w_out, grad_filters)
```

```python
import functools

import jax
import jax.numpy as jnp
from jax import lax
from jax.experimental import pallas as pl
from jax.experimental.pallas import tpu as pltpu
from jax.sharding import PartitionSpec as P

F32 = jnp.float32
BF16 = jnp.bfloat16
LANES = 128


def doc_start(positions, starts):
    before = starts[None, :] <= positions[:, None]
    return jnp.max(jnp.where(before, starts[None, :], 0), axis=1)


def toeplitz(row, rows):
    wide = jnp.broadcast_to(row, (rows, row.shape[-1]))
    return pltpu.roll(wide, 0, 1, stride=1, stride_axis=0)


def group_lanes(rows, per_group, index):
    lane = lax.broadcasted_iota(jnp.int32, (rows, LANES), 1)
    return (lane >= index * per_group) & (lane < (index + 1) * per_group)


def forward_kernel(per_group, q_ref, prev_ref, own_ref, taps_ref, mask_ref, filt_ref, gated_ref):
    rows, width = q_ref.shape
    mask = mask_ref[...].astype(F32)
    per_tile = LANES // per_group
    for tile in range(width // LANES):
        cols = slice(tile * LANES, (tile + 1) * LANES)
        ext = jnp.concatenate([prev_ref[:, cols], own_ref[:, cols]], axis=0)
        acc = jnp.zeros((rows, LANES), F32)
        for g in range(per_tile):
            row = tile * per_tile + g
            band = (toeplitz(taps_ref[row : row + 1, :], rows) * mask).astype(BF16)
            res = jnp.dot(band, ext, preferred_element_type=F32)
            acc = jnp.where(group_lanes(rows, per_group, g), res, acc)
        filt_ref[:, cols] = acc
        gated_ref[:, cols] = (q_ref[:, cols].astype(F32) * acc).astype(BF16)


def backward_kernel(
    per_group, k_ref, v_ref, prev_ref, own_ref, gate_ref, next_ref, grad_in_ref, filt_ref, taps_ref,
    fmask_ref, bmask_ref, gq_ref, gk_ref, gv_ref, sums_ref,
):
    rows, width = k_ref.shape
    bmask = bmask_ref[...].astype(F32)
    fmask = fmask_ref[...].astype(F32)
    per_tile = LANES // per_group
    r = lax.broadcasted_iota(jnp.int32, (rows, rows), 0)
    c = lax.broadcasted_iota(jnp.int32, (rows, rows), 1)
    flip = jnp.where(r + c == rows - 1, 1.0, 0.0).astype(BF16)
    gq_ref[...] = (grad_in_ref[...] * filt_ref[...]).astype(BF16)
    for tile in range(width // LANES):
        cols = slice(tile * LANES, (tile + 1) * LANES)
        gate = gate_ref[:, cols]
        gext = jnp.concatenate([gate, next_ref[:, cols]], axis=0)
        ext = jnp.concatenate([prev_ref[:, cols], own_ref[:, cols]], axis=0)
        turned = jnp.dot(flip, gate, preferred_element_type=F32)
        acc = jnp.zeros((rows, LANES), F32)
        for g in range(per_tile):
            row = tile * per_tile + g
            lanes = group_lanes(rows, per_group, g)
            band = (toeplitz(taps_ref[row : row + 1, :], rows) * bmask).astype(BF16)
            res = jnp.dot(band, gext, preferred_element_type=F32)
            acc = jnp.where(lanes, res, acc)
            mine = jnp.where(lanes, turned, 0.0).astype(BF16)
            pair = lax.dot_general(
                mine, ext, (((1,), (1,)), ((), ())), preferred_element_type=F32
            )
            pair = pltpu.roll(pair * fmask, 0, 1, stride=1, stride_axis=0)
            sums_ref[row : row + 1, :] = jnp.sum(pair, axis=0, keepdims=True)
        gk_ref[:, cols] = (acc * v_ref[:, cols].astype(F32)).astype(BF16)
        gv_ref[:, cols] = (acc * k_ref[:, cols].astype(F32)).astype(BF16)


def body(n_seq, query_in, key_in, value_in, filters, doc_lengths, w_out, cotangent):
    tok_rows, chan_count = query_in.shape
    group_count, length = filters.shape
    per_group = chan_count // group_count
    step = 2 * LANES if chan_count % (2 * LANES) == 0 else LANES
    step_groups = step // per_group
    span = 2 * tok_rows

    full_cot = lax.all_gather(cotangent, "chan", axis=1, tiled=True)

    product_kv = (key_in.astype(F32) * value_in.astype(F32)).astype(BF16)
    up = [(i, i + 1) for i in range(n_seq - 1)]
    down = [(i + 1, i) for i in range(n_seq - 1)]
    prev_kv = lax.ppermute(product_kv, "seq", up)

    starts = jnp.cumsum(doc_lengths) - doc_lengths
    first_row = lax.axis_index("seq") * tok_rows
    wide = jnp.arange(span, dtype=jnp.int32)
    own_pos = first_row + wide[:tok_rows]
    fmask = ((first_row - tok_rows + wide)[None, :] >= doc_start(own_pos, starts)[:, None]).astype(BF16)
    bmask = (own_pos[:, None] >= doc_start(first_row + wide, starts)[None, :]).astype(BF16)
    taps = filters.astype(F32)
    none = jnp.zeros((group_count, span - length), F32)
    back_taps = jnp.concatenate([taps, none], axis=1)
    fore_taps = jnp.roll(jnp.flip(back_taps, 1), tok_rows + 1, axis=1)

    tile = pl.BlockSpec((tok_rows, step), lambda i: (0, i))
    rowspec = pl.BlockSpec((step_groups, span), lambda i: (i, 0))
    whole = pl.BlockSpec((tok_rows, span), lambda i: (0, 0))
    blocks = chan_count // step
    filtered, gated = pl.pallas_call(
        functools.partial(forward_kernel, per_group),
        grid=(blocks,),
        in_specs=[tile, tile, tile, rowspec, whole],
        out_specs=[tile, tile],
        out_shape=[
            jax.ShapeDtypeStruct((tok_rows, chan_count), F32),
            jax.ShapeDtypeStruct((tok_rows, chan_count), BF16),
        ],
    )(query_in, prev_kv, product_kv, fore_taps, fmask)

    gated_all = lax.all_gather(gated, "seq", axis=0, tiled=True)

    grad_in = jnp.einsum("tn,cn->tc", full_cot, w_out, preferred_element_type=F32)
    grad_gate = (grad_in * query_in.astype(F32)).astype(BF16)
    next_gate = lax.ppermute(grad_gate, "seq", down)
    cot_cols = lax.all_to_all(full_cot, "seq", split_axis=1, concat_axis=0, tiled=True)

    partial_out = jnp.dot(gated, w_out, preferred_element_type=F32)
    block_out = lax.psum_scatter(
        partial_out.astype(BF16), "chan", scatter_dimension=1, tiled=True
    )

    grad_query, grad_key, grad_value, sums = pl.pallas_call(
        functools.partial(backward_kernel, per_group),
        grid=(blocks,),
        in_specs=[tile] * 8 + [rowspec, whole, whole],
        out_specs=[tile] * 3 + [rowspec],
        out_shape=[jax.ShapeDtypeStruct((tok_rows, chan_count), BF16)] * 3
        + [jax.ShapeDtypeStruct((group_count, span), F32)],
    )(
        key_in, value_in, prev_kv, product_kv, grad_gate, next_gate, grad_in, filtered,
        back_taps, jnp.flip(fmask, 0), bmask,
    )
    tap_part = jnp.flip(sums[:, span - length :], 1)
    tap_sum = lax.psum_scatter(
        tap_part.astype(BF16), "seq", scatter_dimension=1, tiled=True
    ).astype(F32)

    weight = lax.dot_general(
        gated_all, cot_cols, (((0,), (0,)), ((), ())), preferred_element_type=F32
    ).astype(BF16)
    return (block_out, grad_query, grad_key, grad_value, weight, tap_sum)


def solution(mesh):
    act = P("seq", "chan")
    return jax.shard_map(
        functools.partial(body, mesh.shape["seq"]),
        mesh=mesh,
        in_specs=(act, act, act, P("chan", None), P(), P("chan", None), act),
        out_specs=(act, act, act, act, P("chan", "seq"), P("chan", "seq")),
        check_vma=False,
    )
```

```python
import functools

import jax
import jax.numpy as jnp
from jax import lax
from jax.experimental import pallas as pl
from jax.experimental.pallas import tpu as pltpu
from jax.sharding import PartitionSpec as P

F32 = jnp.float32
BF16 = jnp.bfloat16
LANES = 128


def doc_start(positions, starts):
    before = starts[None, :] <= positions[:, None]
    return jnp.max(jnp.where(before, starts[None, :], 0), axis=1)


def toeplitz(row, rows):
    wide = jnp.broadcast_to(row, (rows, row.shape[-1]))
    return pltpu.roll(wide, 0, 1, stride=1, stride_axis=0)


def group_lanes(rows, per_group, index):
    lane = lax.broadcasted_iota(jnp.int32, (rows, LANES), 1)
    return (lane >= index * per_group) & (lane < (index + 1) * per_group)


def forward_kernel(per_group, q_ref, prev_ref, own_ref, taps_ref, mask_ref, filt_ref, gated_ref):
    rows, width = q_ref.shape
    mask = mask_ref[...].astype(F32)
    per_tile = LANES // per_group
    for tile in range(width // LANES):
        cols = slice(tile * LANES, (tile + 1) * LANES)
        ext = jnp.concatenate([prev_ref[:, cols], own_ref[:, cols]], axis=0)
        acc = jnp.zeros((rows, LANES), F32)
        for g in range(per_tile):
            row = tile * per_tile + g
            band = (toeplitz(taps_ref[row : row + 1, :], rows) * mask).astype(BF16)
            res = jnp.dot(band, ext, preferred_element_type=F32)
            acc = jnp.where(group_lanes(rows, per_group, g), res, acc)
        filt_ref[:, cols] = acc
        gated_ref[:, cols] = (q_ref[:, cols].astype(F32) * acc).astype(BF16)


def backward_kernel(
    per_group, k_ref, v_ref, prev_ref, own_ref, gate_ref, next_ref, grad_in_ref, filt_ref, taps_ref,
    fmask_ref, bmask_ref, gq_ref, gk_ref, gv_ref, sums_ref,
):
    rows, width = k_ref.shape
    bmask = bmask_ref[...].astype(F32)
    fmask = fmask_ref[...].astype(F32)
    per_tile = LANES // per_group
    r = lax.broadcasted_iota(jnp.int32, (rows, rows), 0)
    c = lax.broadcasted_iota(jnp.int32, (rows, rows), 1)
    flip = jnp.where(r + c == rows - 1, 1.0, 0.0).astype(BF16)
    gq_ref[...] = (grad_in_ref[...] * filt_ref[...]).astype(BF16)
    for tile in range(width // LANES):
        cols = slice(tile * LANES, (tile + 1) * LANES)
        gate = gate_ref[:, cols]
        gext = jnp.concatenate([gate, next_ref[:, cols]], axis=0)
        ext = jnp.concatenate([prev_ref[:, cols], own_ref[:, cols]], axis=0)
        turned = jnp.dot(flip, gate, preferred_element_type=F32)
        acc = jnp.zeros((rows, LANES), F32)
        for g in range(per_tile):
            row = tile * per_tile + g
            lanes = group_lanes(rows, per_group, g)
            band = (toeplitz(taps_ref[row : row + 1, :], rows) * bmask).astype(BF16)
            res = jnp.dot(band, gext, preferred_element_type=F32)
            acc = jnp.where(lanes, res, acc)
            mine = jnp.where(lanes, turned, 0.0).astype(BF16)
            pair = lax.dot_general(
                mine, ext, (((1,), (1,)), ((), ())), preferred_element_type=F32
            )
            pair = pltpu.roll(pair * fmask, 0, 1, stride=1, stride_axis=0)
            sums_ref[row : row + 1, :] = jnp.sum(pair, axis=0, keepdims=True)
        gk_ref[:, cols] = (acc * v_ref[:, cols].astype(F32)).astype(BF16)
        gv_ref[:, cols] = (acc * k_ref[:, cols].astype(F32)).astype(BF16)


def prepare(tok_rows, filters, doc_lengths):
    group_count, length = filters.shape
    span = 2 * tok_rows
    starts = jnp.cumsum(doc_lengths) - doc_lengths
    first_row = lax.axis_index("seq") * tok_rows
    wide = jnp.arange(span, dtype=jnp.int32)
    own_pos = first_row + wide[:tok_rows]
    fmask = ((first_row - tok_rows + wide)[None, :] >= doc_start(own_pos, starts)[:, None]).astype(BF16)
    bmask = (own_pos[:, None] >= doc_start(first_row + wide, starts)[None, :]).astype(BF16)
    taps = filters.astype(F32)
    none = jnp.zeros((group_count, span - length), F32)
    back_taps = jnp.concatenate([taps, none], axis=1)
    fore_taps = jnp.roll(jnp.flip(back_taps, 1), tok_rows + 1, axis=1)
    return fore_taps, back_taps, fmask, bmask


def body(n_seq, query_in, key_in, value_in, filters, doc_lengths, w_out, cotangent):
    tok_rows, chan_count = query_in.shape
    group_count, length = filters.shape
    per_group = chan_count // group_count
    step = 2 * LANES if chan_count % (2 * LANES) == 0 else LANES
    step_groups = step // per_group
    span = 2 * tok_rows

    full_cot = lax.all_gather(cotangent, "chan", axis=1, tiled=True)

    product_kv = (key_in.astype(F32) * value_in.astype(F32)).astype(BF16)
    up = [(i, i + 1) for i in range(n_seq - 1)]
    down = [(i + 1, i) for i in range(n_seq - 1)]
    prev_kv = lax.ppermute(product_kv, "seq", up)

    fore_taps, back_taps, fmask, bmask = prepare(tok_rows, filters, doc_lengths)
    tile = pl.BlockSpec((tok_rows, step), lambda i: (0, i))
    rowspec = pl.BlockSpec((step_groups, span), lambda i: (i, 0))
    whole = pl.BlockSpec((tok_rows, span), lambda i: (0, 0))
    blocks = chan_count // step
    filtered, gated = pl.pallas_call(
        functools.partial(forward_kernel, per_group),
        grid=(blocks,),
        in_specs=[tile, tile, tile, rowspec, whole],
        out_specs=[tile, tile],
        out_shape=[
            jax.ShapeDtypeStruct((tok_rows, chan_count), F32),
            jax.ShapeDtypeStruct((tok_rows, chan_count), BF16),
        ],
    )(query_in, prev_kv, product_kv, fore_taps, fmask)

    gated_all = lax.all_gather(gated, "seq", axis=0, tiled=True)

    grad_in = jnp.einsum("tn,cn->tc", full_cot, w_out, preferred_element_type=F32)
    grad_gate = (grad_in * query_in.astype(F32)).astype(BF16)
    next_gate = lax.ppermute(grad_gate, "seq", down)
    cot_cols = lax.all_to_all(full_cot, "seq", split_axis=1, concat_axis=0, tiled=True)

    partial_out = jnp.dot(gated, w_out, preferred_element_type=F32)
    block_out = lax.psum_scatter(
        partial_out.astype(BF16), "chan", scatter_dimension=1, tiled=True
    )

    grad_query, grad_key, grad_value, sums = pl.pallas_call(
        functools.partial(backward_kernel, per_group),
        grid=(blocks,),
        in_specs=[tile] * 8 + [rowspec, whole, whole],
        out_specs=[tile] * 3 + [rowspec],
        out_shape=[jax.ShapeDtypeStruct((tok_rows, chan_count), BF16)] * 3
        + [jax.ShapeDtypeStruct((group_count, span), F32)],
    )(
        key_in, value_in, prev_kv, product_kv, grad_gate, next_gate, grad_in, filtered,
        back_taps, jnp.flip(fmask, 0), bmask,
    )
    tap_part = jnp.flip(sums[:, span - length :], 1)
    tap_sum = lax.psum_scatter(
        tap_part.astype(BF16), "seq", scatter_dimension=1, tiled=True
    ).astype(F32)

    weight = lax.dot_general(
        gated_all, cot_cols, (((0,), (0,)), ((), ())), preferred_element_type=F32
    ).astype(BF16)
    return (block_out, grad_query, grad_key, grad_value, weight, tap_sum)


def mega_kernel(
    per_group, n_seq, n_chan, q_ref, k_ref, v_ref, cot_ref, fore_ref, back_ref, fmask_ref, rmask_ref,
    bmask_ref, w_hbm, out_ref, gq_ref, gk_ref, gv_ref, gw_ref, tap_ref,
    w_ref, kv_ref, prev_ref, gate_ref, next_ref, filt_ref, gin_ref, gall_ref, cots_ref, cotc_ref,
    psend_ref, precv_ref, tsend_ref, trecv_ref, sums_ref,
    w_sem, rim_send, rim_recv, cot_send, cot_recv, part_send, part_recv, a2a_send, a2a_recv,
    share_send, share_recv, tap_send, tap_recv, line_send, line_recv, pair_send, pair_recv,
):
    rows, width = q_ref.shape
    block = gw_ref.shape[1]
    per_chan = width // block
    half = rows // 2
    tiles = width // LANES
    per_tile = LANES // per_group
    s = lax.axis_index("seq")
    c = lax.axis_index("chan")
    hops = n_seq // 2
    z = s // 2
    pair = s + 1 - 2 * (s % 2)
    mate = c + 1 - 2 * (c % 2)
    core = c % 2

    def remote(src, dst, send, recv, seq, chan):
        return pltpu.make_async_remote_copy(
            src_ref=src, dst_ref=dst, send_sem=send, recv_sem=recv,
            device_id=(seq, chan), device_id_type=pl.DeviceIdType.MESH,
        )

    w_copy = pltpu.make_async_copy(w_hbm, w_ref, w_sem)
    w_copy.start()

    barrier = pltpu.get_barrier_semaphore()
    for o in range(1, n_seq):
        pl.semaphore_signal(
            barrier, inc=1, device_id=(lax.rem(s + o, n_seq), c),
            device_id_type=pl.DeviceIdType.MESH,
        )
    for o in range(1, n_chan):
        pl.semaphore_signal(
            barrier, inc=1, device_id=(s, lax.rem(c + o, n_chan)),
            device_id_type=pl.DeviceIdType.MESH,
        )
    kv_ref[...] = (k_ref[...].astype(F32) * v_ref[...].astype(F32)).astype(BF16)
    cots_ref[c] = cot_ref[...]
    pl.semaphore_wait(barrier, n_seq + n_chan - 2)

    def rim(index, src, dst, to):
        return remote(src, dst, rim_send.at[index], rim_recv.at[index], to, c)

    @pl.when(s < n_seq - 1)
    def _():
        rim(0, kv_ref, prev_ref, s + 1).start()

    def cot_copy(o):
        return remote(
            cot_ref, cots_ref.at[c], cot_send.at[o], cot_recv.at[o], s, lax.rem(c + o, n_chan)
        )

    for o in range(1, n_chan):
        cot_copy(o).start()

    @pl.when(s == 0)
    def _():
        prev_ref[...] = jnp.zeros_like(prev_ref)

    @pl.when(s == n_seq - 1)
    def _():
        next_ref[...] = jnp.zeros_like(next_ref)

    @pl.when(s > 0)
    def _():
        rim(0, kv_ref, prev_ref, s).wait_recv()

    own_rows = pl.ds(pl.multiple_of(s * rows, rows), rows)

    @pl.loop(0, tiles)
    def _(tile):
        cols = pl.ds(pl.multiple_of(tile * LANES, LANES), LANES)
        mask = fmask_ref[...].astype(F32)
        taps = fore_ref[pl.ds(pl.multiple_of(tile * per_tile, per_tile), per_tile), :]
        ext = jnp.concatenate([prev_ref[:, cols], kv_ref[:, cols]], axis=0)
        acc = jnp.zeros((rows, LANES), F32)
        for g in range(per_tile):
            band = (toeplitz(taps[g : g + 1, :], rows) * mask).astype(BF16)
            res = jnp.dot(band, ext, preferred_element_type=F32)
            acc = jnp.where(group_lanes(rows, per_group, g), res, acc)
        filt_ref[:, cols] = acc
        gall_ref[own_rows, cols] = (q_ref[:, cols].astype(F32) * acc).astype(BF16)

    def line(side, h, seq):
        rows_of = pl.ds(pl.multiple_of(seq * rows, rows), rows)
        to = s + 2 if side == 0 else s - 2
        return remote(
            gall_ref.at[rows_of, :], gall_ref.at[rows_of, :],
            line_send.at[side, h], line_recv.at[side, h], to, c,
        )

    def across(side, h, seq):
        rows_of = pl.ds(pl.multiple_of(seq * rows, rows), rows)
        return remote(
            gall_ref.at[rows_of, :], gall_ref.at[rows_of, :],
            pair_send.at[side, h], pair_recv.at[side, h], pair, c,
        )

    def pass_on(h):
        up, down = s - 2 * h, s + 2 * h
        if h > 0:
            @pl.when(z - h >= 0)
            def _():
                line(0, h - 1, up).wait_recv()

        @pl.when((z - h >= 0) & (z < hops - 1))
        def _():
            line(0, h, up).start()

        @pl.when(z - h >= 0)
        def _():
            across(0, h, up).start()

        if h > 0:
            @pl.when(z + h < hops)
            def _():
                line(1, h - 1, down).wait_recv()

        @pl.when((z + h < hops) & (z > 0))
        def _():
            line(1, h, down).start()

        if h > 0:
            @pl.when(z + h < hops)
            def _():
                across(1, h, down).start()

    pass_on(0)

    w_copy.wait()
    for o in range(1, n_chan):
        cot_copy(o).wait_recv()

    def a2a_copy(o):
        to = lax.rem(s + o, n_seq)
        half_rows = pl.ds(pl.multiple_of(core * half, half), half)
        src = cots_ref.at[
            to // per_chan, half_rows, pl.ds(pl.multiple_of((to % per_chan) * block, block), block)
        ]
        dst = cotc_ref.at[pl.ds(pl.multiple_of(s * rows + core * half, half), half), :]
        return remote(src, dst, a2a_send.at[o], a2a_recv.at[o], to, c)

    for o in range(1, n_seq):
        a2a_copy(o).start()

    in_tile = 2 * LANES

    @pl.loop(0, width // in_tile)
    def _(tile):
        cols = pl.ds(pl.multiple_of(tile * in_tile, in_tile), in_tile)
        acc = jnp.zeros((rows, in_tile), F32)
        for p in range(n_chan):
            acc = acc + lax.dot_general(
                cots_ref[p], w_ref[cols, p * width : (p + 1) * width],
                (((1,), (1,)), ((), ())), preferred_element_type=F32,
            )
        gin_ref[:, cols] = acc
        gate_ref[:, cols] = (acc * q_ref[:, cols].astype(F32)).astype(BF16)

    @pl.when(s > 0)
    def _():
        rim(1, gate_ref, next_ref, s - 1).start()

    cotc_ref[own_rows, :] = cots_ref[
        s // per_chan, :, pl.ds(pl.multiple_of((s % per_chan) * block, block), block)
    ]
    pass_on(1)

    def part_copy(o):
        to = lax.rem(c + o, n_chan)
        return remote(
            psend_ref.at[to], precv_ref.at[c], part_send.at[o], part_recv.at[o], s, to
        )

    gated = gall_ref.at[own_rows, :]
    for o in range(1, n_chan + 1):
        to = lax.rem(c + o, n_chan)
        dest = psend_ref if o < n_chan else precv_ref

        @pl.loop(0, width // in_tile)
        def _(tile):
            cols = pl.ds(pl.multiple_of(tile * in_tile, in_tile), in_tile)
            w_cols = pl.ds(pl.multiple_of(to * width + tile * in_tile, in_tile), in_tile)
            dest[to, :, cols] = jnp.dot(
                gated[...], w_ref[:, w_cols], preferred_element_type=F32
            ).astype(BF16)

        if o < n_chan:
            part_copy(o).start()

    for h in range(2, hops - 1):
        pass_on(h)

    def share_copy(o):
        came = lax.rem(s + n_seq - o, n_seq)
        at = pl.ds(pl.multiple_of(came * rows + core * half, half), half)
        return remote(
            cotc_ref.at[at, :], cotc_ref.at[at, :], share_send.at[o], share_recv.at[o], s, mate
        )

    @pl.when(s < n_seq - 1)
    def _():
        rim(1, gate_ref, next_ref, s).wait_recv()

    r = lax.broadcasted_iota(jnp.int32, (rows, rows), 0)
    cc = lax.broadcasted_iota(jnp.int32, (rows, rows), 1)
    turn = jnp.where(r + cc == rows - 1, 1.0, 0.0).astype(BF16)

    @pl.loop(0, tiles)
    def _(tile):
        cols = pl.ds(pl.multiple_of(tile * LANES, LANES), LANES)
        at = pl.ds(pl.multiple_of(tile * per_tile, per_tile), per_tile)
        bmask = bmask_ref[...].astype(F32)
        rmask = rmask_ref[...].astype(F32)
        taps = back_ref[at, :]
        gate = gate_ref[:, cols]
        gext = jnp.concatenate([gate, next_ref[:, cols]], axis=0)
        ext = jnp.concatenate([prev_ref[:, cols], kv_ref[:, cols]], axis=0)
        turned = jnp.dot(turn, gate, preferred_element_type=F32)
        acc = jnp.zeros((rows, LANES), F32)
        found = []
        for g in range(per_tile):
            lanes = group_lanes(rows, per_group, g)
            band = (toeplitz(taps[g : g + 1, :], rows) * bmask).astype(BF16)
            res = jnp.dot(band, gext, preferred_element_type=F32)
            acc = jnp.where(lanes, res, acc)
            mine = jnp.where(lanes, turned, 0.0).astype(BF16)
            terms = lax.dot_general(
                mine, ext, (((1,), (1,)), ((), ())), preferred_element_type=F32
            )
            terms = pltpu.roll(terms * rmask, 0, 1, stride=1, stride_axis=0)
            found.append(jnp.sum(terms, axis=0, keepdims=True))
        sums_ref[at, :] = jnp.concatenate(found, axis=0)
        gq_ref[:, cols] = (gin_ref[:, cols] * filt_ref[:, cols]).astype(BF16)
        gk_ref[:, cols] = (acc * v_ref[:, cols].astype(F32)).astype(BF16)
        gv_ref[:, cols] = (acc * k_ref[:, cols].astype(F32)).astype(BF16)

    tsend_ref[...] = sums_ref[:, sums_ref.shape[1] - LANES :].astype(BF16)

    def tap_copy(o):
        return remote(
            tsend_ref, trecv_ref.at[s], tap_send.at[o], tap_recv.at[o], lax.rem(s + o, n_seq), c
        )

    for o in range(1, n_seq):
        tap_copy(o).start()
    trecv_ref[s] = tsend_ref[...]

    for o in range(1, n_seq):
        a2a_copy(o).wait_recv()
        share_copy(o).start()
    for h in range(max(2, hops - 1), hops):
        pass_on(h)

    for o in range(1, n_chan):
        part_copy(o).wait_recv()

    @pl.loop(0, width // in_tile)
    def _(tile):
        cols = pl.ds(pl.multiple_of(tile * in_tile, in_tile), in_tile)
        acc = precv_ref[0, :, cols].astype(F32)
        for p in range(1, n_chan):
            acc = acc + precv_ref[p, :, cols].astype(F32)
        out_ref[:, cols] = acc.astype(BF16)

    for o in range(1, n_seq):
        tap_copy(o).wait_recv()
    total = trecv_ref[0].astype(F32)
    for p in range(1, n_seq):
        total = total + trecv_ref[p].astype(F32)
    tap_ref[...] = total

    for o in range(1, n_seq):
        share_copy(o).wait_recv()
    for h in range(hops):
        @pl.when(z - h >= 0)
        def _():
            across(0, h, s - 2 * h).wait_recv()

        if h > 0:
            @pl.when(z + h < hops)
            def _():
                across(1, h, s + 2 * h).wait_recv()

    @pl.loop(0, width // in_tile)
    def _(tile):
        cols = pl.ds(pl.multiple_of(tile * in_tile, in_tile), in_tile)
        gw_ref[cols, :] = lax.dot_general(
            gall_ref[:, cols], cotc_ref[...], (((0,), (0,)), ((), ())),
            preferred_element_type=F32,
        ).astype(BF16)

    @pl.when(s < n_seq - 1)
    def _():
        rim(0, kv_ref, prev_ref, s + 1).wait_send()

    @pl.when(s > 0)
    def _():
        rim(1, gate_ref, next_ref, s - 1).wait_send()

    for o in range(1, n_chan):
        cot_copy(o).wait_send()
        part_copy(o).wait_send()
    for o in range(1, n_seq):
        a2a_copy(o).wait_send()
        share_copy(o).wait_send()
        tap_copy(o).wait_send()
    for h in range(hops):
        @pl.when((z - h >= 0) & (z < hops - 1))
        def _():
            line(0, h, s - 2 * h).wait_send()

        @pl.when((z + h < hops) & (z > 0))
        def _():
            line(1, h, s + 2 * h).wait_send()

        @pl.when(z - h >= 0)
        def _():
            across(0, h, s - 2 * h).wait_send()

        if h > 0:
            @pl.when(z + h < hops)
            def _():
                across(1, h, s + 2 * h).wait_send()


def fused_body(n_seq, n_chan, query_in, key_in, value_in, filters, doc_lengths, w_out, cotangent):
    rows, width = query_in.shape
    groups, length = filters.shape
    per_group = width // groups
    block = w_out.shape[1] // n_seq
    fore_taps, back_taps, fmask, bmask = prepare(rows, filters, doc_lengths)
    vmem = pl.BlockSpec(memory_space=pltpu.VMEM)
    act = jax.ShapeDtypeStruct((rows, width), BF16)
    dma = pltpu.SemaphoreType.DMA
    hops = n_seq // 2
    block_out, grad_query, grad_key, grad_value, weight, taps = pl.pallas_call(
        functools.partial(mega_kernel, per_group, n_seq, n_chan),
        in_specs=[vmem] * 9 + [pl.BlockSpec(memory_space=pl.ANY)],
        out_specs=[vmem] * 6,
        out_shape=[act] * 4
        + [
            jax.ShapeDtypeStruct((width, block), BF16),
            jax.ShapeDtypeStruct((groups, length), F32),
        ],
        scratch_shapes=[
            pltpu.VMEM(w_out.shape, BF16),
            pltpu.VMEM((rows, width), BF16),
            pltpu.VMEM((rows, width), BF16),
            pltpu.VMEM((rows, width), BF16),
            pltpu.VMEM((rows, width), BF16),
            pltpu.VMEM((rows, width), F32),
            pltpu.VMEM((rows, width), F32),
            pltpu.VMEM((n_seq * rows, width), BF16),
            pltpu.VMEM((n_chan, rows, width), BF16),
            pltpu.VMEM((n_seq * rows, block), BF16),
            pltpu.VMEM((n_chan, rows, width), BF16),
            pltpu.VMEM((n_chan, rows, width), BF16),
            pltpu.VMEM((groups, length), BF16),
            pltpu.VMEM((n_seq, groups, length), BF16),
            pltpu.VMEM((groups, 2 * rows), F32),
            dma, dma((2,)), dma((2,)), dma((n_chan,)), dma((n_chan,)), dma((n_chan,)),
            dma((n_chan,)), dma((n_seq,)), dma((n_seq,)), dma((n_seq,)), dma((n_seq,)),
            dma((n_seq,)), dma((n_seq,)), dma((2, hops)), dma((2, hops)), dma((2, hops)),
            dma((2, hops)),
        ],
        compiler_params=pltpu.CompilerParams(
            collective_id=0, has_side_effects=True, vmem_limit_bytes=56 * 2**20
        ),
    )(
        query_in, key_in, value_in, cotangent, fore_taps, back_taps, fmask, jnp.flip(fmask, 0),
        bmask, w_out,
    )
    share = length // n_seq
    at = length - (lax.axis_index("seq") + 1) * share
    tap_sum = jnp.flip(lax.dynamic_slice_in_dim(taps, at, share, axis=1), 1)
    return (block_out, grad_query, grad_key, grad_value, weight, tap_sum)


def program(n_seq, n_chan, *arrays):
    rows, width = arrays[0].shape
    groups, length = arrays[3].shape
    block = arrays[5].shape[1] // n_seq
    aligned = block % LANES == 0 and width % block == 0 and width % (2 * LANES) == 0
    even = n_seq % 2 == 0 and n_chan % 2 == 0 and n_seq >= 4
    if aligned and even and rows == length == LANES and LANES * groups % width == 0:
        return fused_body(n_seq, n_chan, *arrays)
    return body(n_seq, *arrays)


def solution(mesh):
    act = P("seq", "chan")
    return jax.shard_map(
        functools.partial(program, mesh.shape["seq"], mesh.shape["chan"]),
        mesh=mesh,
        in_specs=(act, act, act, P("chan", None), P(), P("chan", None), act),
        out_specs=(act, act, act, act, P("chan", "seq"), P("chan", "seq")),
        check_vma=False,
    )
```

```python
import functools

import jax
import jax.numpy as jnp
from jax import lax
from jax.experimental import pallas as pl
from jax.experimental.pallas import tpu as pltpu
from jax.sharding import PartitionSpec as P

F32 = jnp.float32
BF16 = jnp.bfloat16
LANES = 128


def doc_start(positions, starts):
    before = starts[None, :] <= positions[:, None]
    return jnp.max(jnp.where(before, starts[None, :], 0), axis=1)


def toeplitz(row, rows, shift=0):
    wide = jnp.broadcast_to(row, (rows, row.shape[-1]))
    return pltpu.roll(wide, shift, 1, stride=1, stride_axis=0)


def group_lanes(rows, per_group, index):
    lane = lax.broadcasted_iota(jnp.int32, (rows, LANES), 1)
    return (lane >= index * per_group) & (lane < (index + 1) * per_group)


def forward_kernel(per_group, q_ref, prev_ref, own_ref, taps_ref, mask_ref, filt_ref, gated_ref):
    rows, width = q_ref.shape
    mask = mask_ref[...].astype(F32)
    per_tile = LANES // per_group
    for tile in range(width // LANES):
        cols = slice(tile * LANES, (tile + 1) * LANES)
        ext = jnp.concatenate([prev_ref[:, cols], own_ref[:, cols]], axis=0)
        acc = jnp.zeros((rows, LANES), F32)
        for g in range(per_tile):
            row = tile * per_tile + g
            band = (toeplitz(taps_ref[row : row + 1, :], rows) * mask).astype(BF16)
            res = jnp.dot(band, ext, preferred_element_type=F32)
            acc = jnp.where(group_lanes(rows, per_group, g), res, acc)
        filt_ref[:, cols] = acc
        gated_ref[:, cols] = (q_ref[:, cols].astype(F32) * acc).astype(BF16)


def backward_kernel(
    per_group, k_ref, v_ref, prev_ref, own_ref, gate_ref, next_ref, grad_in_ref, filt_ref, taps_ref,
    fmask_ref, bmask_ref, gq_ref, gk_ref, gv_ref, sums_ref,
):
    rows, width = k_ref.shape
    bmask = bmask_ref[...].astype(F32)
    fmask = fmask_ref[...].astype(F32)
    per_tile = LANES // per_group
    r = lax.broadcasted_iota(jnp.int32, (rows, rows), 0)
    c = lax.broadcasted_iota(jnp.int32, (rows, rows), 1)
    flip = jnp.where(r + c == rows - 1, 1.0, 0.0).astype(BF16)
    gq_ref[...] = (grad_in_ref[...] * filt_ref[...]).astype(BF16)
    for tile in range(width // LANES):
        cols = slice(tile * LANES, (tile + 1) * LANES)
        gate = gate_ref[:, cols]
        gext = jnp.concatenate([gate, next_ref[:, cols]], axis=0)
        ext = jnp.concatenate([prev_ref[:, cols], own_ref[:, cols]], axis=0)
        turned = jnp.dot(flip, gate, preferred_element_type=F32)
        acc = jnp.zeros((rows, LANES), F32)
        for g in range(per_tile):
            row = tile * per_tile + g
            lanes = group_lanes(rows, per_group, g)
            band = (toeplitz(taps_ref[row : row + 1, :], rows) * bmask).astype(BF16)
            res = jnp.dot(band, gext, preferred_element_type=F32)
            acc = jnp.where(lanes, res, acc)
            mine = jnp.where(lanes, turned, 0.0).astype(BF16)
            pair = lax.dot_general(
                mine, ext, (((1,), (1,)), ((), ())), preferred_element_type=F32
            )
            pair = pltpu.roll(pair * fmask, 0, 1, stride=1, stride_axis=0)
            sums_ref[row : row + 1, :] = jnp.sum(pair, axis=0, keepdims=True)
        gk_ref[:, cols] = (acc * v_ref[:, cols].astype(F32)).astype(BF16)
        gv_ref[:, cols] = (acc * k_ref[:, cols].astype(F32)).astype(BF16)


def prepare(tok_rows, filters, doc_lengths):
    group_count, length = filters.shape
    span = 2 * tok_rows
    starts = jnp.cumsum(doc_lengths) - doc_lengths
    first_row = lax.axis_index("seq") * tok_rows
    wide = jnp.arange(span, dtype=jnp.int32)
    own_pos = first_row + wide[:tok_rows]
    fmask = ((first_row - tok_rows + wide)[None, :] >= doc_start(own_pos, starts)[:, None]).astype(BF16)
    bmask = (own_pos[:, None] >= doc_start(first_row + wide, starts)[None, :]).astype(BF16)
    taps = filters.astype(F32)
    none = jnp.zeros((group_count, span - length), F32)
    back_taps = jnp.concatenate([taps, none], axis=1)
    fore_taps = jnp.roll(jnp.flip(back_taps, 1), tok_rows + 1, axis=1)
    return fore_taps, back_taps, fmask, bmask


def body(n_seq, query_in, key_in, value_in, filters, doc_lengths, w_out, cotangent):
    tok_rows, chan_count = query_in.shape
    group_count, length = filters.shape
    per_group = chan_count // group_count
    step = 2 * LANES if chan_count % (2 * LANES) == 0 else LANES
    step_groups = step // per_group
    span = 2 * tok_rows

    full_cot = lax.all_gather(cotangent, "chan", axis=1, tiled=True)

    product_kv = (key_in.astype(F32) * value_in.astype(F32)).astype(BF16)
    up = [(i, i + 1) for i in range(n_seq - 1)]
    down = [(i + 1, i) for i in range(n_seq - 1)]
    prev_kv = lax.ppermute(product_kv, "seq", up)

    fore_taps, back_taps, fmask, bmask = prepare(tok_rows, filters, doc_lengths)
    tile = pl.BlockSpec((tok_rows, step), lambda i: (0, i))
    rowspec = pl.BlockSpec((step_groups, span), lambda i: (i, 0))
    whole = pl.BlockSpec((tok_rows, span), lambda i: (0, 0))
    blocks = chan_count // step
    filtered, gated = pl.pallas_call(
        functools.partial(forward_kernel, per_group),
        grid=(blocks,),
        in_specs=[tile, tile, tile, rowspec, whole],
        out_specs=[tile, tile],
        out_shape=[
            jax.ShapeDtypeStruct((tok_rows, chan_count), F32),
            jax.ShapeDtypeStruct((tok_rows, chan_count), BF16),
        ],
    )(query_in, prev_kv, product_kv, fore_taps, fmask)

    gated_all = lax.all_gather(gated, "seq", axis=0, tiled=True)

    grad_in = jnp.einsum("tn,cn->tc", full_cot, w_out, preferred_element_type=F32)
    grad_gate = (grad_in * query_in.astype(F32)).astype(BF16)
    next_gate = lax.ppermute(grad_gate, "seq", down)
    cot_cols = lax.all_to_all(full_cot, "seq", split_axis=1, concat_axis=0, tiled=True)

    partial_out = jnp.dot(gated, w_out, preferred_element_type=F32)
    block_out = lax.psum_scatter(
        partial_out.astype(BF16), "chan", scatter_dimension=1, tiled=True
    )

    grad_query, grad_key, grad_value, sums = pl.pallas_call(
        functools.partial(backward_kernel, per_group),
        grid=(blocks,),
        in_specs=[tile] * 8 + [rowspec, whole, whole],
        out_specs=[tile] * 3 + [rowspec],
        out_shape=[jax.ShapeDtypeStruct((tok_rows, chan_count), BF16)] * 3
        + [jax.ShapeDtypeStruct((group_count, span), F32)],
    )(
        key_in, value_in, prev_kv, product_kv, grad_gate, next_gate, grad_in, filtered,
        back_taps, jnp.flip(fmask, 0), bmask,
    )
    tap_part = jnp.flip(sums[:, span - length :], 1)
    tap_sum = lax.psum_scatter(
        tap_part.astype(BF16), "seq", scatter_dimension=1, tiled=True
    ).astype(F32)

    weight = lax.dot_general(
        gated_all, cot_cols, (((0,), (0,)), ((), ())), preferred_element_type=F32
    ).astype(BF16)
    return (block_out, grad_query, grad_key, grad_value, weight, tap_sum)


def mega_kernel(
    per_group, n_seq, n_chan, chunks, q_ref, k_ref, v_ref, cot_ref, taps_ref, len_ref, w_hbm,
    out_ref, gq_ref, gk_ref, gv_ref, gw_ref, tap_ref,
    w_ref, kv_ref, prev_ref, gate_ref, next_ref, filt_ref, gin_ref, gall_ref, cots_ref, cotc_ref,
    psend_ref, precv_ref, tsend_ref, trecv_ref, sums_ref, fore_ref, back_ref, fmask_ref, rmask_ref, bmask_ref,
    w_sem, rim_send, rim_recv, cot_send, cot_recv, pass_send, pass_recv, part_send, part_recv,
    a2a_send, a2a_recv, share_send, share_recv, tap_send, tap_recv, line_send, line_recv,
    pair_send, pair_recv,
):
    rows, width = q_ref.shape
    span = 2 * rows
    block = gw_ref.shape[1]
    per_chan = width // block
    half = rows // 2
    per_tile = LANES // per_group
    piece = width // chunks
    piece_tiles = piece // LANES
    s = lax.axis_index("seq")
    c = lax.axis_index("chan")
    hops = n_seq // 2
    z = s // 2
    pair = s + 1 - 2 * (s % 2)
    mate = c + 1 - 2 * (c % 2)
    core = c % 2

    def remote(src, dst, send, recv, seq, chan):
        return pltpu.make_async_remote_copy(
            src_ref=src, dst_ref=dst, send_sem=send, recv_sem=recv,
            device_id=(seq, chan), device_id_type=pl.DeviceIdType.MESH,
        )

    w_copy = pltpu.make_async_copy(w_hbm, w_ref, w_sem)
    w_copy.start()

    barrier = pltpu.get_barrier_semaphore()
    for o in range(1, n_seq):
        pl.semaphore_signal(
            barrier, inc=1, device_id=(lax.rem(s + o, n_seq), c),
            device_id_type=pl.DeviceIdType.MESH,
        )
    for o in range(1, n_chan):
        pl.semaphore_signal(
            barrier, inc=1, device_id=(s, lax.rem(c + o, n_chan)),
            device_id_type=pl.DeviceIdType.MESH,
        )
    kv_ref[...] = (k_ref[...].astype(F32) * v_ref[...].astype(F32)).astype(BF16)
    cots_ref[c] = cot_ref[...]

    row = lax.broadcasted_iota(jnp.int32, (rows, span), 0) + s * rows
    lane = lax.broadcasted_iota(jnp.int32, (rows, span), 1) + s * rows
    turned_row = 2 * s * rows + rows - 1 - row

    def first(pos):
        best = jnp.zeros_like(pos)
        start = jnp.int32(0)
        for d in range(len_ref.shape[0]):
            best = jnp.where(start <= pos, start, best)
            start = start + len_ref[d]
        return best

    fmask_ref[...] = jnp.where(lane - rows >= first(row), 1.0, 0.0)
    rmask_ref[...] = jnp.where(lane - rows >= first(turned_row), 1.0, 0.0)
    bmask_ref[...] = jnp.where(row >= first(lane), 1.0, 0.0)
    r = lax.broadcasted_iota(jnp.int32, (rows, rows), 0)
    cc = lax.broadcasted_iota(jnp.int32, (rows, rows), 1)
    turn = jnp.where(r + cc == rows - 1, 1.0, 0.0).astype(BF16)
    back_ref[...] = taps_ref[...].astype(F32)
    fore_ref[...] = jnp.dot(taps_ref[...], turn, preferred_element_type=F32)

    @pl.when(s == 0)
    def _():
        prev_ref[...] = jnp.zeros_like(prev_ref)

    @pl.when(s == n_seq - 1)
    def _():
        next_ref[...] = jnp.zeros_like(next_ref)

    pl.semaphore_wait(barrier, n_seq + n_chan - 2)

    def rim(index, src, dst, ch, to):
        cols = pl.ds(ch * piece, piece)
        return remote(
            src.at[:, cols], dst.at[:, cols], rim_send.at[index, ch], rim_recv.at[index, ch], to, c
        )

    @pl.when(s < n_seq - 1)
    def _():
        for ch in range(chunks):
            rim(0, kv_ref, prev_ref, ch, s + 1).start()

    def cot_copy(o):
        to = mate if o == 0 else lax.rem(c + 2 * o, n_chan)
        return remote(cot_ref, cots_ref.at[c], cot_send.at[o], cot_recv.at[o], s, to)

    def cot_pass(o):
        came = lax.rem(c + n_chan - 2 * o, n_chan)
        return remote(
            cots_ref.at[came], cots_ref.at[came], pass_send.at[o], pass_recv.at[o], s, mate
        )

    chips = n_chan // 2
    for o in range(1, chips):
        cot_copy(o).start()
    cot_copy(0).start()

    own_rows = pl.ds(pl.multiple_of(s * rows, rows), rows)

    def line(side, h, ch, seq):
        rows_of = pl.ds(pl.multiple_of(seq * rows, rows), rows)
        part = gall_ref.at[rows_of, pl.ds(ch * piece, piece)]
        to = s + 2 if side == 0 else s - 2
        return remote(part, part, line_send.at[side, h, ch], line_recv.at[side, h, ch], to, c)

    def across(side, h, ch, seq):
        rows_of = pl.ds(pl.multiple_of(seq * rows, rows), rows)
        part = gall_ref.at[rows_of, pl.ds(ch * piece, piece)]
        return remote(part, part, pair_send.at[side, h, ch], pair_recv.at[side, h, ch], pair, c)

    def pass_on(h, ch):
        up, down = s - 2 * h, s + 2 * h
        if h > 0:
            @pl.when(z - h >= 0)
            def _():
                line(0, h - 1, ch, up).wait_recv()

        @pl.when((z - h >= 0) & (z < hops - 1))
        def _():
            line(0, h, ch, up).start()

        @pl.when(z - h >= 0)
        def _():
            across(0, h, ch, up).start()

        if h > 0:
            @pl.when(z + h < hops)
            def _():
                line(1, h - 1, ch, down).wait_recv()

        @pl.when((z + h < hops) & (z > 0))
        def _():
            line(1, h, ch, down).start()

        if h > 0:
            @pl.when(z + h < hops)
            def _():
                across(1, h, ch, down).start()

    for ch in range(chunks):
        @pl.when(s > 0)
        def _():
            rim(0, kv_ref, prev_ref, ch, s).wait_recv()

        @pl.loop(ch * piece_tiles, (ch + 1) * piece_tiles)
        def _(tile):
            cols = pl.ds(pl.multiple_of(tile * LANES, LANES), LANES)
            mask = fmask_ref[...]
            taps = fore_ref[pl.ds(pl.multiple_of(tile * per_tile, per_tile), per_tile), :]
            taps = jnp.concatenate([taps, jnp.zeros_like(taps)], axis=1)
            ext = jnp.concatenate([prev_ref[:, cols], kv_ref[:, cols]], axis=0)
            acc = jnp.zeros((rows, LANES), F32)
            for g in range(per_tile):
                band = (toeplitz(taps[g : g + 1, :], rows, 1) * mask).astype(BF16)
                res = jnp.dot(band, ext, preferred_element_type=F32)
                acc = jnp.where(group_lanes(rows, per_group, g), res, acc)
            filt_ref[:, cols] = acc
            gall_ref[own_rows, cols] = (q_ref[:, cols].astype(F32) * acc).astype(BF16)

        pass_on(0, ch)

    for o in range(1, chips):
        cot_copy(o).wait_recv()
        cot_pass(o).start()
    cot_copy(0).wait_recv()
    w_copy.wait()
    for o in range(1, chips):
        cot_pass(o).wait_recv()

    def a2a_copy(o):
        to = lax.rem(s + o, n_seq)
        half_rows = pl.ds(pl.multiple_of(core * half, half), half)
        src = cots_ref.at[
            to // per_chan, half_rows, pl.ds(pl.multiple_of((to % per_chan) * block, block), block)
        ]
        dst = cotc_ref.at[pl.ds(pl.multiple_of(s * rows + core * half, half), half), :]
        return remote(src, dst, a2a_send.at[o], a2a_recv.at[o], to, c)

    for o in range(1, n_seq):
        a2a_copy(o).start()

    in_tile = 2 * LANES
    piece_ins = piece // in_tile

    for ch in range(chunks):
        @pl.loop(ch * piece_ins, (ch + 1) * piece_ins)
        def _(tile):
            cols = pl.ds(pl.multiple_of(tile * in_tile, in_tile), in_tile)
            acc = jnp.zeros((rows, in_tile), F32)
            for p in range(n_chan):
                acc = acc + lax.dot_general(
                    cots_ref[p], w_ref[cols, p * width : (p + 1) * width],
                    (((1,), (1,)), ((), ())), preferred_element_type=F32,
                )
            gin_ref[:, cols] = acc
            gate_ref[:, cols] = (acc * q_ref[:, cols].astype(F32)).astype(BF16)

        @pl.when(s > 0)
        def _():
            rim(1, gate_ref, next_ref, ch, s - 1).start()

        pass_on(1, ch)

    cotc_ref[own_rows, :] = cots_ref[
        s // per_chan, :, pl.ds(pl.multiple_of((s % per_chan) * block, block), block)
    ]

    def part_copy(o):
        to = lax.rem(c + o, n_chan)
        return remote(
            psend_ref.at[to], precv_ref.at[c], part_send.at[o], part_recv.at[o], s, to
        )

    gated = gall_ref.at[own_rows, :]
    later = [(h, ch) for h in range(2, hops) for ch in range(chunks)]
    waiting = later[:chunks]
    for o in range(1, n_chan + 1):
        to = lax.rem(c + o, n_chan)
        dest = psend_ref if o < n_chan else precv_ref

        @pl.loop(0, width // in_tile)
        def _(tile):
            cols = pl.ds(pl.multiple_of(tile * in_tile, in_tile), in_tile)
            w_cols = pl.ds(pl.multiple_of(to * width + tile * in_tile, in_tile), in_tile)
            dest[to, :, cols] = jnp.dot(
                gated[...], w_ref[:, w_cols], preferred_element_type=F32
            ).astype(BF16)

        if o < n_chan:
            part_copy(o).start()
        if waiting:
            pass_on(*waiting.pop(0))
    for left in waiting:
        pass_on(*left)

    def share_copy(o):
        came = lax.rem(s + n_seq - o, n_seq)
        at = pl.ds(pl.multiple_of(came * rows + core * half, half), half)
        return remote(
            cotc_ref.at[at, :], cotc_ref.at[at, :], share_send.at[o], share_recv.at[o], s, mate
        )

    waiting = later[chunks:]
    for ch in range(chunks):
        @pl.when(s < n_seq - 1)
        def _():
            rim(1, gate_ref, next_ref, ch, s).wait_recv()

        @pl.loop(ch * piece_tiles, (ch + 1) * piece_tiles)
        def _(tile):
            cols = pl.ds(pl.multiple_of(tile * LANES, LANES), LANES)
            at = pl.ds(pl.multiple_of(tile * per_tile, per_tile), per_tile)
            bmask = bmask_ref[...]
            rmask = rmask_ref[...]
            taps = back_ref[at, :]
            taps = jnp.concatenate([taps, jnp.zeros_like(taps)], axis=1)
            gate = gate_ref[:, cols]
            gext = jnp.concatenate([gate, next_ref[:, cols]], axis=0)
            ext = jnp.concatenate([prev_ref[:, cols], kv_ref[:, cols]], axis=0)
            turned = jnp.dot(turn, gate, preferred_element_type=F32)
            acc = jnp.zeros((rows, LANES), F32)
            found = []
            for g in range(per_tile):
                lanes = group_lanes(rows, per_group, g)
                band = (toeplitz(taps[g : g + 1, :], rows) * bmask).astype(BF16)
                res = jnp.dot(band, gext, preferred_element_type=F32)
                acc = jnp.where(lanes, res, acc)
                mine = jnp.where(lanes, turned, 0.0).astype(BF16)
                terms = lax.dot_general(
                    mine, ext, (((1,), (1,)), ((), ())), preferred_element_type=F32
                )
                terms = pltpu.roll(terms * rmask, 0, 1, stride=1, stride_axis=0)
                found.append(jnp.sum(terms, axis=0, keepdims=True))
            sums_ref[at, :] = jnp.concatenate(found, axis=0)
            gq_ref[:, cols] = (gin_ref[:, cols] * filt_ref[:, cols]).astype(BF16)
            gk_ref[:, cols] = (acc * v_ref[:, cols].astype(F32)).astype(BF16)
            gv_ref[:, cols] = (acc * k_ref[:, cols].astype(F32)).astype(BF16)

        if waiting:
            pass_on(*waiting.pop(0))
    for left in waiting:
        pass_on(*left)

    tsend_ref[...] = jnp.dot(
        sums_ref[:, span - LANES :].astype(BF16), turn, preferred_element_type=F32
    ).astype(BF16)

    def tap_copy(o):
        return remote(
            tsend_ref, trecv_ref.at[s], tap_send.at[o], tap_recv.at[o], lax.rem(s + o, n_seq), c
        )

    for o in range(1, n_seq):
        tap_copy(o).start()
    trecv_ref[s] = tsend_ref[...]

    for o in range(1, n_seq):
        a2a_copy(o).wait_recv()
        share_copy(o).start()

    for o in range(1, n_chan):
        part_copy(o).wait_recv()

    @pl.loop(0, width // in_tile)
    def _(tile):
        cols = pl.ds(pl.multiple_of(tile * in_tile, in_tile), in_tile)
        acc = precv_ref[0, :, cols].astype(F32)
        for p in range(1, n_chan):
            acc = acc + precv_ref[p, :, cols].astype(F32)
        out_ref[:, cols] = acc.astype(BF16)

    for o in range(1, n_seq):
        tap_copy(o).wait_recv()
    total = trecv_ref[0].astype(F32)
    for p in range(1, n_seq):
        total = total + trecv_ref[p].astype(F32)
    share = tap_ref.shape[1]
    total = pltpu.roll(total, lax.rem(LANES - s * share, LANES), 1)
    tap_ref[...] = total[:, :share]

    for o in range(1, n_seq):
        share_copy(o).wait_recv()
    for ch in range(chunks):
        for h in range(hops):
            @pl.when(z - h >= 0)
            def _():
                across(0, h, ch, s - 2 * h).wait_recv()

            if h > 0:
                @pl.when(z + h < hops)
                def _():
                    across(1, h, ch, s + 2 * h).wait_recv()

        @pl.loop(ch * piece_ins, (ch + 1) * piece_ins)
        def _(tile):
            cols = pl.ds(pl.multiple_of(tile * in_tile, in_tile), in_tile)
            gw_ref[cols, :] = lax.dot_general(
                gall_ref[:, cols], cotc_ref[...], (((0,), (0,)), ((), ())),
                preferred_element_type=F32,
            ).astype(BF16)

    for ch in range(chunks):
        @pl.when(s < n_seq - 1)
        def _():
            rim(0, kv_ref, prev_ref, ch, s + 1).wait_send()

        @pl.when(s > 0)
        def _():
            rim(1, gate_ref, next_ref, ch, s - 1).wait_send()

    for o in range(chips):
        cot_copy(o).wait_send()
    for o in range(1, chips):
        cot_pass(o).wait_send()
    for o in range(1, n_chan):
        part_copy(o).wait_send()
    for o in range(1, n_seq):
        a2a_copy(o).wait_send()
        share_copy(o).wait_send()
        tap_copy(o).wait_send()
    for h in range(hops):
        for ch in range(chunks):
            @pl.when((z - h >= 0) & (z < hops - 1))
            def _():
                line(0, h, ch, s - 2 * h).wait_send()

            @pl.when((z + h < hops) & (z > 0))
            def _():
                line(1, h, ch, s + 2 * h).wait_send()

            @pl.when(z - h >= 0)
            def _():
                across(0, h, ch, s - 2 * h).wait_send()

            if h > 0:
                @pl.when(z + h < hops)
                def _():
                    across(1, h, ch, s + 2 * h).wait_send()


def fused_body(n_seq, n_chan, query_in, key_in, value_in, filters, doc_lengths, w_out, cotangent):
    rows, width = query_in.shape
    groups, length = filters.shape
    per_group = width // groups
    block = w_out.shape[1] // n_seq
    ins = width // (2 * LANES)
    chunks = 3 if ins % 3 == 0 else 2 if ins % 2 == 0 else 1
    vmem = pl.BlockSpec(memory_space=pltpu.VMEM)
    act = jax.ShapeDtypeStruct((rows, width), BF16)
    dma = pltpu.SemaphoreType.DMA
    hops = n_seq // 2
    results = pl.pallas_call(
        functools.partial(mega_kernel, per_group, n_seq, n_chan, chunks),
        in_specs=[vmem] * 5
        + [pl.BlockSpec(memory_space=pltpu.SMEM), pl.BlockSpec(memory_space=pl.ANY)],
        out_specs=[vmem] * 6,
        out_shape=[act] * 4
        + [
            jax.ShapeDtypeStruct((width, block), BF16),
            jax.ShapeDtypeStruct((groups, length // n_seq), F32),
        ],
        scratch_shapes=[
            pltpu.VMEM(w_out.shape, BF16),
            pltpu.VMEM((rows, width), BF16),
            pltpu.VMEM((rows, width), BF16),
            pltpu.VMEM((rows, width), BF16),
            pltpu.VMEM((rows, width), BF16),
            pltpu.VMEM((rows, width), F32),
            pltpu.VMEM((rows, width), F32),
            pltpu.VMEM((n_seq * rows, width), BF16),
            pltpu.VMEM((n_chan, rows, width), BF16),
            pltpu.VMEM((n_seq * rows, block), BF16),
            pltpu.VMEM((n_chan, rows, width), BF16),
            pltpu.VMEM((n_chan, rows, width), BF16),
            pltpu.VMEM((groups, length), BF16),
            pltpu.VMEM((n_seq, groups, length), BF16),
            pltpu.VMEM((groups, 2 * rows), F32),
            pltpu.VMEM((groups, length), F32),
            pltpu.VMEM((groups, length), F32),
            pltpu.VMEM((rows, 2 * rows), F32),
            pltpu.VMEM((rows, 2 * rows), F32),
            pltpu.VMEM((rows, 2 * rows), F32),
            dma, dma((2, chunks)), dma((2, chunks)), dma((n_chan,)), dma((n_chan,)),
            dma((n_chan,)), dma((n_chan,)), dma((n_chan,)), dma((n_chan,)), dma((n_seq,)),
            dma((n_seq,)), dma((n_seq,)), dma((n_seq,)), dma((n_seq,)), dma((n_seq,)),
            dma((2, hops, chunks)), dma((2, hops, chunks)), dma((2, hops, chunks)),
            dma((2, hops, chunks)),
        ],
        compiler_params=pltpu.CompilerParams(
            collective_id=0, has_side_effects=True, vmem_limit_bytes=56 * 2**20
        ),
    )(query_in, key_in, value_in, cotangent, filters, doc_lengths, w_out)
    return tuple(results)


def program(n_seq, n_chan, *arrays):
    rows, width = arrays[0].shape
    groups, length = arrays[3].shape
    block = arrays[5].shape[1] // n_seq
    aligned = block % LANES == 0 and width % block == 0 and width % (2 * LANES) == 0
    even = n_seq % 2 == 0 and n_chan % 2 == 0 and n_seq >= 4
    if aligned and even and rows == length == LANES and LANES * groups % width == 0:
        return fused_body(n_seq, n_chan, *arrays)
    return body(n_seq, *arrays)


def solution(mesh):
    act = P("seq", "chan")
    return jax.shard_map(
        functools.partial(program, mesh.shape["seq"], mesh.shape["chan"]),
        mesh=mesh,
        in_specs=(act, act, act, P("chan", None), P(), P("chan", None), act),
        out_specs=(act, act, act, act, P("chan", "seq"), P("chan", "seq")),
        check_vma=False,
    )
```

```python
import functools

import jax
import jax.numpy as jnp
from jax import lax
from jax.experimental import pallas as pl
from jax.experimental.pallas import tpu as pltpu
from jax.sharding import PartitionSpec as P

F32 = jnp.float32
BF16 = jnp.bfloat16
LANES = 128


def doc_start(positions, starts):
    before = starts[None, :] <= positions[:, None]
    return jnp.max(jnp.where(before, starts[None, :], 0), axis=1)


def toeplitz(row, rows, shift=0):
    wide = jnp.broadcast_to(row, (rows, row.shape[-1]))
    return pltpu.roll(wide, shift, 1, stride=1, stride_axis=0)


def group_lanes(rows, per_group, index):
    lane = lax.broadcasted_iota(jnp.int32, (rows, LANES), 1)
    return (lane >= index * per_group) & (lane < (index + 1) * per_group)


def forward_kernel(per_group, q_ref, prev_ref, own_ref, taps_ref, mask_ref, filt_ref, gated_ref):
    rows, width = q_ref.shape
    mask = mask_ref[...].astype(F32)
    per_tile = LANES // per_group
    for tile in range(width // LANES):
        cols = slice(tile * LANES, (tile + 1) * LANES)
        ext = jnp.concatenate([prev_ref[:, cols], own_ref[:, cols]], axis=0)
        acc = jnp.zeros((rows, LANES), F32)
        for g in range(per_tile):
            row = tile * per_tile + g
            band = (toeplitz(taps_ref[row : row + 1, :], rows) * mask).astype(BF16)
            res = jnp.dot(band, ext, preferred_element_type=F32)
            acc = jnp.where(group_lanes(rows, per_group, g), res, acc)
        filt_ref[:, cols] = acc
        gated_ref[:, cols] = (q_ref[:, cols].astype(F32) * acc).astype(BF16)


def backward_kernel(
    per_group, k_ref, v_ref, prev_ref, own_ref, gate_ref, next_ref, grad_in_ref, filt_ref, taps_ref,
    fmask_ref, bmask_ref, gq_ref, gk_ref, gv_ref, sums_ref,
):
    rows, width = k_ref.shape
    bmask = bmask_ref[...].astype(F32)
    fmask = fmask_ref[...].astype(F32)
    per_tile = LANES // per_group
    r = lax.broadcasted_iota(jnp.int32, (rows, rows), 0)
    c = lax.broadcasted_iota(jnp.int32, (rows, rows), 1)
    flip = jnp.where(r + c == rows - 1, 1.0, 0.0).astype(BF16)
    gq_ref[...] = (grad_in_ref[...] * filt_ref[...]).astype(BF16)
    for tile in range(width // LANES):
        cols = slice(tile * LANES, (tile + 1) * LANES)
        gate = gate_ref[:, cols]
        gext = jnp.concatenate([gate, next_ref[:, cols]], axis=0)
        ext = jnp.concatenate([prev_ref[:, cols], own_ref[:, cols]], axis=0)
        turned = jnp.dot(flip, gate, preferred_element_type=F32)
        acc = jnp.zeros((rows, LANES), F32)
        for g in range(per_tile):
            row = tile * per_tile + g
            lanes = group_lanes(rows, per_group, g)
            band = (toeplitz(taps_ref[row : row + 1, :], rows) * bmask).astype(BF16)
            res = jnp.dot(band, gext, preferred_element_type=F32)
            acc = jnp.where(lanes, res, acc)
            mine = jnp.where(lanes, turned, 0.0).astype(BF16)
            pair = lax.dot_general(
                mine, ext, (((1,), (1,)), ((), ())), preferred_element_type=F32
            )
            pair = pltpu.roll(pair * fmask, 0, 1, stride=1, stride_axis=0)
            sums_ref[row : row + 1, :] = jnp.sum(pair, axis=0, keepdims=True)
        gk_ref[:, cols] = (acc * v_ref[:, cols].astype(F32)).astype(BF16)
        gv_ref[:, cols] = (acc * k_ref[:, cols].astype(F32)).astype(BF16)


def prepare(tok_rows, filters, doc_lengths):
    group_count, length = filters.shape
    span = 2 * tok_rows
    starts = jnp.cumsum(doc_lengths) - doc_lengths
    first_row = lax.axis_index("seq") * tok_rows
    wide = jnp.arange(span, dtype=jnp.int32)
    own_pos = first_row + wide[:tok_rows]
    fmask = ((first_row - tok_rows + wide)[None, :] >= doc_start(own_pos, starts)[:, None]).astype(BF16)
    bmask = (own_pos[:, None] >= doc_start(first_row + wide, starts)[None, :]).astype(BF16)
    taps = filters.astype(F32)
    none = jnp.zeros((group_count, span - length), F32)
    back_taps = jnp.concatenate([taps, none], axis=1)
    fore_taps = jnp.roll(jnp.flip(back_taps, 1), tok_rows + 1, axis=1)
    return fore_taps, back_taps, fmask, bmask


def body(n_seq, query_in, key_in, value_in, filters, doc_lengths, w_out, cotangent):
    tok_rows, chan_count = query_in.shape
    group_count, length = filters.shape
    per_group = chan_count // group_count
    step = 2 * LANES if chan_count % (2 * LANES) == 0 else LANES
    step_groups = step // per_group
    span = 2 * tok_rows

    full_cot = lax.all_gather(cotangent, "chan", axis=1, tiled=True)

    product_kv = (key_in.astype(F32) * value_in.astype(F32)).astype(BF16)
    up = [(i, i + 1) for i in range(n_seq - 1)]
    down = [(i + 1, i) for i in range(n_seq - 1)]
    prev_kv = lax.ppermute(product_kv, "seq", up)

    fore_taps, back_taps, fmask, bmask = prepare(tok_rows, filters, doc_lengths)
    tile = pl.BlockSpec((tok_rows, step), lambda i: (0, i))
    rowspec = pl.BlockSpec((step_groups, span), lambda i: (i, 0))
    whole = pl.BlockSpec((tok_rows, span), lambda i: (0, 0))
    blocks = chan_count // step
    filtered, gated = pl.pallas_call(
        functools.partial(forward_kernel, per_group),
        grid=(blocks,),
        in_specs=[tile, tile, tile, rowspec, whole],
        out_specs=[tile, tile],
        out_shape=[
            jax.ShapeDtypeStruct((tok_rows, chan_count), F32),
            jax.ShapeDtypeStruct((tok_rows, chan_count), BF16),
        ],
    )(query_in, prev_kv, product_kv, fore_taps, fmask)

    gated_all = lax.all_gather(gated, "seq", axis=0, tiled=True)

    grad_in = jnp.einsum("tn,cn->tc", full_cot, w_out, preferred_element_type=F32)
    grad_gate = (grad_in * query_in.astype(F32)).astype(BF16)
    next_gate = lax.ppermute(grad_gate, "seq", down)
    cot_cols = lax.all_to_all(full_cot, "seq", split_axis=1, concat_axis=0, tiled=True)

    partial_out = jnp.dot(gated, w_out, preferred_element_type=F32)
    block_out = lax.psum_scatter(
        partial_out.astype(BF16), "chan", scatter_dimension=1, tiled=True
    )

    grad_query, grad_key, grad_value, sums = pl.pallas_call(
        functools.partial(backward_kernel, per_group),
        grid=(blocks,),
        in_specs=[tile] * 8 + [rowspec, whole, whole],
        out_specs=[tile] * 3 + [rowspec],
        out_shape=[jax.ShapeDtypeStruct((tok_rows, chan_count), BF16)] * 3
        + [jax.ShapeDtypeStruct((group_count, span), F32)],
    )(
        key_in, value_in, prev_kv, product_kv, grad_gate, next_gate, grad_in, filtered,
        back_taps, jnp.flip(fmask, 0), bmask,
    )
    tap_part = jnp.flip(sums[:, span - length :], 1)
    tap_sum = lax.psum_scatter(
        tap_part.astype(BF16), "seq", scatter_dimension=1, tiled=True
    ).astype(F32)

    weight = lax.dot_general(
        gated_all, cot_cols, (((0,), (0,)), ((), ())), preferred_element_type=F32
    ).astype(BF16)
    return (block_out, grad_query, grad_key, grad_value, weight, tap_sum)


def mega_kernel(
    per_group, n_seq, n_chan, chunks, q_ref, k_ref, v_ref, cot_ref, taps_ref, len_ref, w_hbm,
    out_ref, gq_ref, gk_ref, gv_ref, gw_ref, tap_ref,
    w_ref, kv_ref, prev_ref, gate_ref, next_ref, filt_ref, gin_ref, gall_ref, cots_ref, cotc_ref,
    psend_ref, precv_ref, tsend_ref, trecv_ref, sums_ref, fore_ref, back_ref, fmask_ref, rmask_ref,
    bmask_ref,
    w_sem, rim_send, rim_recv, cot_send, cot_recv, pass_send, pass_recv, part_send, part_recv,
    a2a_send, a2a_recv, share_send, share_recv, tap_send, tap_recv, line_send, line_recv,
    pair_send, pair_recv,
):
    rows, width = q_ref.shape
    span = 2 * rows
    block = gw_ref.shape[1]
    per_chan = width // block
    share_rows = rows // n_chan
    per_tile = LANES // per_group
    piece = width // chunks
    piece_tiles = piece // LANES
    s = lax.axis_index("seq")
    c = lax.axis_index("chan")
    hops = n_seq // 2
    z = s // 2
    pair = s + 1 - 2 * (s % 2)
    mate = c + 1 - 2 * (c % 2)

    def remote(src, dst, send, recv, seq, chan):
        return pltpu.make_async_remote_copy(
            src_ref=src, dst_ref=dst, send_sem=send, recv_sem=recv,
            device_id=(seq, chan), device_id_type=pl.DeviceIdType.MESH,
        )

    w_copy = pltpu.make_async_copy(w_hbm, w_ref, w_sem)
    w_copy.start()

    barrier = pltpu.get_barrier_semaphore()
    for o in range(1, n_seq):
        pl.semaphore_signal(
            barrier, inc=1, device_id=(lax.rem(s + o, n_seq), c),
            device_id_type=pl.DeviceIdType.MESH,
        )
    for o in range(1, n_chan):
        pl.semaphore_signal(
            barrier, inc=1, device_id=(s, lax.rem(c + o, n_chan)),
            device_id_type=pl.DeviceIdType.MESH,
        )
    kv_ref[...] = (k_ref[...].astype(F32) * v_ref[...].astype(F32)).astype(BF16)
    cots_ref[c] = cot_ref[...]

    row = lax.broadcasted_iota(jnp.int32, (rows, span), 0) + s * rows
    lane = lax.broadcasted_iota(jnp.int32, (rows, span), 1) + s * rows
    turned_row = 2 * s * rows + rows - 1 - row

    def first(pos):
        best = jnp.zeros_like(pos)
        start = jnp.int32(0)
        for d in range(len_ref.shape[0]):
            best = jnp.where(start <= pos, start, best)
            start = start + len_ref[d]
        return best

    fmask_ref[...] = jnp.where(lane - rows >= first(row), 1.0, 0.0)
    rmask_ref[...] = jnp.where(lane - rows >= first(turned_row), 1.0, 0.0)
    bmask_ref[...] = jnp.where(row >= first(lane), 1.0, 0.0)
    r = lax.broadcasted_iota(jnp.int32, (rows, rows), 0)
    cc = lax.broadcasted_iota(jnp.int32, (rows, rows), 1)
    turn = jnp.where(r + cc == rows - 1, 1.0, 0.0).astype(BF16)
    back_ref[...] = taps_ref[...].astype(F32)
    fore_ref[...] = jnp.dot(taps_ref[...], turn, preferred_element_type=F32)

    @pl.when(s == 0)
    def _():
        prev_ref[...] = jnp.zeros_like(prev_ref)

    @pl.when(s == n_seq - 1)
    def _():
        next_ref[...] = jnp.zeros_like(next_ref)

    pl.semaphore_wait(barrier, n_seq + n_chan - 2)

    def rim(index, src, dst, ch, to):
        cols = pl.ds(ch * piece, piece)
        return remote(
            src.at[:, cols], dst.at[:, cols], rim_send.at[index, ch], rim_recv.at[index, ch], to, c
        )

    @pl.when(s < n_seq - 1)
    def _():
        for ch in range(chunks):
            rim(0, kv_ref, prev_ref, ch, s + 1).start()

    def cot_copy(o):
        to = mate if o == 0 else lax.rem(c + 2 * o, n_chan)
        return remote(cot_ref, cots_ref.at[c], cot_send.at[o], cot_recv.at[o], s, to)

    def cot_pass(o):
        came = lax.rem(c + n_chan - 2 * o, n_chan)
        return remote(
            cots_ref.at[came], cots_ref.at[came], pass_send.at[o], pass_recv.at[o], s, mate
        )

    chips = n_chan // 2
    for o in range(1, chips):
        cot_copy(o).start()
    cot_copy(0).start()

    own_rows = pl.ds(pl.multiple_of(s * rows, rows), rows)

    def line(side, h, ch, seq, other=0):
        rows_of = pl.ds(pl.multiple_of(seq * rows, rows), rows)
        part = gall_ref.at[rows_of, pl.ds(ch * piece, piece)]
        to = s + 2 if side == 0 else s - 2
        at = h + other * hops
        return remote(part, part, line_send.at[side, at, ch], line_recv.at[side, at, ch], to, c)

    def across(side, h, ch, seq):
        rows_of = pl.ds(pl.multiple_of(seq * rows, rows), rows)
        part = gall_ref.at[rows_of, pl.ds(ch * piece, piece)]
        return remote(part, part, pair_send.at[side, h, ch], pair_recv.at[side, h, ch], pair, c)

    def pass_both(h, other):
        base = pair if other else s
        up, down = base - 2 * h, base + 2 * h
        if h == 0 and other:
            across(0, 0, 0, s).wait_recv()
        if h > 0:
            @pl.when(z - h >= 0)
            def _():
                line(0, h - 1, 0, up, other).wait_recv()

        @pl.when((z - h >= 0) & (z < hops - 1))
        def _():
            line(0, h, 0, up, other).start()

        if h > 0:
            @pl.when(z + h < hops)
            def _():
                line(1, h - 1, 0, down, other).wait_recv()

        @pl.when((z + h < hops) & (z > 0))
        def _():
            line(1, h, 0, down, other).start()

    def pass_on(h, ch):
        if ch == 0:
            if h == 0:
                across(0, 0, 0, s).start()
                pass_both(0, 0)
            else:
                pass_both(h, 0)
                pass_both(h, 1)
            return
        up, down = s - 2 * h, s + 2 * h
        if h > 0:
            @pl.when(z - h >= 0)
            def _():
                line(0, h - 1, ch, up).wait_recv()

        @pl.when((z - h >= 0) & (z < hops - 1))
        def _():
            line(0, h, ch, up).start()

        @pl.when(z - h >= 0)
        def _():
            across(0, h, ch, up).start()

        if h > 0:
            @pl.when(z + h < hops)
            def _():
                line(1, h - 1, ch, down).wait_recv()

        @pl.when((z + h < hops) & (z > 0))
        def _():
            line(1, h, ch, down).start()

        if h > 0:
            @pl.when(z + h < hops)
            def _():
                across(1, h, ch, down).start()

    for ch in range(chunks):
        @pl.when(s > 0)
        def _():
            rim(0, kv_ref, prev_ref, ch, s).wait_recv()

        @pl.loop(ch * piece_tiles, (ch + 1) * piece_tiles)
        def _(tile):
            cols = pl.ds(pl.multiple_of(tile * LANES, LANES), LANES)
            mask = fmask_ref[...]
            taps = fore_ref[pl.ds(pl.multiple_of(tile * per_tile, per_tile), per_tile), :]
            taps = jnp.concatenate([taps, jnp.zeros_like(taps)], axis=1)
            ext = jnp.concatenate([prev_ref[:, cols], kv_ref[:, cols]], axis=0)
            acc = jnp.zeros((rows, LANES), F32)
            for g in range(per_tile):
                band = (toeplitz(taps[g : g + 1, :], rows, 1) * mask).astype(BF16)
                res = jnp.dot(band, ext, preferred_element_type=F32)
                acc = jnp.where(group_lanes(rows, per_group, g), res, acc)
            filt_ref[:, cols] = acc
            gall_ref[own_rows, cols] = (q_ref[:, cols].astype(F32) * acc).astype(BF16)

        pass_on(0, ch)
        if ch == min(1, chunks - 1):
            pass_both(0, 1)

    for o in range(1, chips):
        cot_copy(o).wait_recv()
        cot_pass(o).start()
    cot_copy(0).wait_recv()
    w_copy.wait()
    for o in range(1, chips):
        cot_pass(o).wait_recv()

    def a2a_copy(o):
        to = lax.rem(s + o, n_seq)
        my_rows = pl.ds(pl.multiple_of(c * share_rows, share_rows), share_rows)
        src = cots_ref.at[
            to // per_chan, my_rows, pl.ds(pl.multiple_of((to % per_chan) * block, block), block)
        ]
        at = pl.multiple_of(s * rows + c * share_rows, share_rows)
        dst = cotc_ref.at[pl.ds(at, share_rows), :]
        return remote(src, dst, a2a_send.at[o], a2a_recv.at[o], to, c)

    for o in range(1, n_seq):
        a2a_copy(o).start()

    in_tile = 2 * LANES
    piece_ins = piece // in_tile

    for ch in range(chunks):
        @pl.loop(ch * piece_ins, (ch + 1) * piece_ins)
        def _(tile):
            cols = pl.ds(pl.multiple_of(tile * in_tile, in_tile), in_tile)
            acc = jnp.zeros((rows, in_tile), F32)
            for p in range(n_chan):
                acc = acc + lax.dot_general(
                    cots_ref[p], w_ref[cols, p * width : (p + 1) * width],
                    (((1,), (1,)), ((), ())), preferred_element_type=F32,
                )
            gin_ref[:, cols] = acc
            gate_ref[:, cols] = (acc * q_ref[:, cols].astype(F32)).astype(BF16)

        @pl.when(s > 0)
        def _():
            rim(1, gate_ref, next_ref, ch, s - 1).start()

        pass_on(1, ch)

    cotc_ref[own_rows, :] = cots_ref[
        s // per_chan, :, pl.ds(pl.multiple_of((s % per_chan) * block, block), block)
    ]

    def part_copy(o):
        to = lax.rem(c + o, n_chan)
        return remote(
            psend_ref.at[to], precv_ref.at[c], part_send.at[o], part_recv.at[o], s, to
        )

    gated = gall_ref.at[own_rows, :]
    later = [(h, ch) for h in range(2, hops) for ch in range(chunks)]
    waiting = later[:chunks]
    for o in range(1, n_chan + 1):
        to = lax.rem(c + o, n_chan)
        dest = psend_ref if o < n_chan else precv_ref

        @pl.loop(0, width // in_tile)
        def _(tile):
            cols = pl.ds(pl.multiple_of(tile * in_tile, in_tile), in_tile)
            w_cols = pl.ds(pl.multiple_of(to * width + tile * in_tile, in_tile), in_tile)
            dest[to, :, cols] = jnp.dot(
                gated[...], w_ref[:, w_cols], preferred_element_type=F32
            ).astype(BF16)

        if o < n_chan:
            part_copy(o).start()
        if waiting:
            pass_on(*waiting.pop(0))
    for left in waiting:
        pass_on(*left)

    def share_copy(o, peer):
        came = lax.rem(s + n_seq - o, n_seq)
        at = pl.multiple_of(came * rows + c * share_rows, share_rows)
        part = cotc_ref.at[pl.ds(at, share_rows), :]
        return remote(
            part, part, share_send.at[o, peer], share_recv.at[o, peer], s,
            lax.rem(c + peer, n_chan),
        )

    waiting = later[chunks:]
    for ch in range(chunks):
        @pl.when(s < n_seq - 1)
        def _():
            rim(1, gate_ref, next_ref, ch, s).wait_recv()

        @pl.loop(ch * piece_tiles, (ch + 1) * piece_tiles)
        def _(tile):
            cols = pl.ds(pl.multiple_of(tile * LANES, LANES), LANES)
            at = pl.ds(pl.multiple_of(tile * per_tile, per_tile), per_tile)
            bmask = bmask_ref[...]
            rmask = rmask_ref[...]
            taps = back_ref[at, :]
            taps = jnp.concatenate([taps, jnp.zeros_like(taps)], axis=1)
            gate = gate_ref[:, cols]
            gext = jnp.concatenate([gate, next_ref[:, cols]], axis=0)
            ext = jnp.concatenate([prev_ref[:, cols], kv_ref[:, cols]], axis=0)
            turned = jnp.dot(turn, gate, preferred_element_type=F32)
            acc = jnp.zeros((rows, LANES), F32)
            found = []
            for g in range(per_tile):
                lanes = group_lanes(rows, per_group, g)
                band = (toeplitz(taps[g : g + 1, :], rows) * bmask).astype(BF16)
                res = jnp.dot(band, gext, preferred_element_type=F32)
                acc = jnp.where(lanes, res, acc)
                mine = jnp.where(lanes, turned, 0.0).astype(BF16)
                terms = lax.dot_general(
                    mine, ext, (((1,), (1,)), ((), ())), preferred_element_type=F32
                )
                terms = pltpu.roll(terms * rmask, 0, 1, stride=1, stride_axis=0)
                found.append(jnp.sum(terms, axis=0, keepdims=True))
            sums_ref[at, :] = jnp.concatenate(found, axis=0)
            gq_ref[:, cols] = (gin_ref[:, cols] * filt_ref[:, cols]).astype(BF16)
            gk_ref[:, cols] = (acc * v_ref[:, cols].astype(F32)).astype(BF16)
            gv_ref[:, cols] = (acc * k_ref[:, cols].astype(F32)).astype(BF16)

        if waiting:
            pass_on(*waiting.pop(0))
    for left in waiting:
        pass_on(*left)

    tsend_ref[...] = jnp.dot(
        sums_ref[:, span - LANES :].astype(BF16), turn, preferred_element_type=F32
    ).astype(BF16)

    def tap_copy(o):
        return remote(
            tsend_ref, trecv_ref.at[s], tap_send.at[o], tap_recv.at[o], lax.rem(s + o, n_seq), c
        )

    for o in range(1, n_seq):
        tap_copy(o).start()
    trecv_ref[s] = tsend_ref[...]

    for o in range(1, n_seq):
        a2a_copy(o).wait_recv()
        for peer in range(1, n_chan):
            share_copy(o, peer).start()

    for o in range(1, n_chan):
        part_copy(o).wait_recv()

    @pl.loop(0, width // in_tile)
    def _(tile):
        cols = pl.ds(pl.multiple_of(tile * in_tile, in_tile), in_tile)
        acc = precv_ref[0, :, cols].astype(F32)
        for p in range(1, n_chan):
            acc = acc + precv_ref[p, :, cols].astype(F32)
        out_ref[:, cols] = acc.astype(BF16)

    for o in range(1, n_seq):
        tap_copy(o).wait_recv()
    total = trecv_ref[0].astype(F32)
    for p in range(1, n_seq):
        total = total + trecv_ref[p].astype(F32)
    share = tap_ref.shape[1]
    total = pltpu.roll(total, lax.rem(LANES - s * share, LANES), 1)
    tap_ref[...] = total[:, :share]

    for o in range(1, n_seq):
        for peer in range(1, n_chan):
            share_copy(o, peer).wait_recv()
    for ch in range(chunks):
        for h in range(hops if ch else 0):
            @pl.when(z - h >= 0)
            def _():
                across(0, h, ch, s - 2 * h).wait_recv()

            if h > 0:
                @pl.when(z + h < hops)
                def _():
                    across(1, h, ch, s + 2 * h).wait_recv()

        @pl.loop(ch * piece_ins, (ch + 1) * piece_ins)
        def _(tile):
            cols = pl.ds(pl.multiple_of(tile * in_tile, in_tile), in_tile)
            gw_ref[cols, :] = lax.dot_general(
                gall_ref[:, cols], cotc_ref[...], (((0,), (0,)), ((), ())),
                preferred_element_type=F32,
            ).astype(BF16)

    for ch in range(chunks):
        @pl.when(s < n_seq - 1)
        def _():
            rim(0, kv_ref, prev_ref, ch, s + 1).wait_send()

        @pl.when(s > 0)
        def _():
            rim(1, gate_ref, next_ref, ch, s - 1).wait_send()

    for o in range(chips):
        cot_copy(o).wait_send()
    for o in range(1, chips):
        cot_pass(o).wait_send()
    for o in range(1, n_chan):
        part_copy(o).wait_send()
    for o in range(1, n_seq):
        a2a_copy(o).wait_send()
        for peer in range(1, n_chan):
            share_copy(o, peer).wait_send()
        tap_copy(o).wait_send()
    across(0, 0, 0, s).wait_send()
    for h in range(hops):
        for other in range(2):
            base = pair if other else s

            @pl.when((z - h >= 0) & (z < hops - 1))
            def _():
                line(0, h, 0, base - 2 * h, other).wait_send()

            @pl.when((z + h < hops) & (z > 0))
            def _():
                line(1, h, 0, base + 2 * h, other).wait_send()

        for ch in range(1, chunks):
            @pl.when((z - h >= 0) & (z < hops - 1))
            def _():
                line(0, h, ch, s - 2 * h).wait_send()

            @pl.when((z + h < hops) & (z > 0))
            def _():
                line(1, h, ch, s + 2 * h).wait_send()

            @pl.when(z - h >= 0)
            def _():
                across(0, h, ch, s - 2 * h).wait_send()

            if h > 0:
                @pl.when(z + h < hops)
                def _():
                    across(1, h, ch, s + 2 * h).wait_send()


def hand_over(*refs):
    big = (len(refs) - 4) // 3
    ins, tap_in = refs[:big], refs[big]
    outs, tap_out = refs[big + 1 : 2 * big + 1], refs[2 * big + 1]
    held, in_sem, out_sem = refs[2 * big + 2 : 3 * big + 2], refs[-2], refs[-1]
    loads = [pltpu.make_async_copy(ins[i], held[i], in_sem.at[i]) for i in range(big)]
    stores = [pltpu.make_async_copy(held[i], outs[i], out_sem.at[i]) for i in range(big)]
    for load in loads:
        load.start()
    tap_out[...] = tap_in[...]
    for load, store in zip(loads, stores):
        load.wait()
        store.start()
    for store in stores:
        store.wait()


def fused_body(n_seq, n_chan, query_in, key_in, value_in, filters, doc_lengths, w_out, cotangent):
    rows, width = query_in.shape
    groups, length = filters.shape
    per_group = width // groups
    block = w_out.shape[1] // n_seq
    ins = width // (2 * LANES)
    chunks = 3 if ins % 3 == 0 else 2 if ins % 2 == 0 else 1
    vmem = pl.BlockSpec(memory_space=pltpu.VMEM)
    act = jax.ShapeDtypeStruct((rows, width), BF16)
    dma = pltpu.SemaphoreType.DMA
    hops = n_seq // 2
    results = pl.pallas_call(
        functools.partial(mega_kernel, per_group, n_seq, n_chan, chunks),
        in_specs=[vmem] * 5
        + [pl.BlockSpec(memory_space=pltpu.SMEM), pl.BlockSpec(memory_space=pl.ANY)],
        out_specs=[vmem] * 6,
        out_shape=[act] * 4
        + [
            jax.ShapeDtypeStruct((width, block), BF16),
            jax.ShapeDtypeStruct((groups, length // n_seq), F32),
        ],
        scratch_shapes=[
            pltpu.VMEM(w_out.shape, BF16),
            pltpu.VMEM((rows, width), BF16),
            pltpu.VMEM((rows, width), BF16),
            pltpu.VMEM((rows, width), BF16),
            pltpu.VMEM((rows, width), BF16),
            pltpu.VMEM((rows, width), F32),
            pltpu.VMEM((rows, width), F32),
            pltpu.VMEM((n_seq * rows, width), BF16),
            pltpu.VMEM((n_chan, rows, width), BF16),
            pltpu.VMEM((n_seq * rows, block), BF16),
            pltpu.VMEM((n_chan, rows, width), BF16),
            pltpu.VMEM((n_chan, rows, width), BF16),
            pltpu.VMEM((groups, length), BF16),
            pltpu.VMEM((n_seq, groups, length), BF16),
            pltpu.VMEM((groups, 2 * rows), F32),
            pltpu.VMEM((groups, length), F32),
            pltpu.VMEM((groups, length), F32),
            pltpu.VMEM((rows, 2 * rows), F32),
            pltpu.VMEM((rows, 2 * rows), F32),
            pltpu.VMEM((rows, 2 * rows), F32),
            dma, dma((2, chunks)), dma((2, chunks)), dma((n_chan,)), dma((n_chan,)),
            dma((n_chan,)), dma((n_chan,)), dma((n_chan,)), dma((n_chan,)), dma((n_seq,)),
            dma((n_seq,)), dma((n_seq, n_chan)), dma((n_seq, n_chan)), dma((n_seq,)),
            dma((n_seq,)), dma((2, 2 * hops, chunks)), dma((2, 2 * hops, chunks)),
            dma((2, hops, chunks)),
            dma((2, hops, chunks)),
        ],
        compiler_params=pltpu.CompilerParams(
            collective_id=0, has_side_effects=True, vmem_limit_bytes=56 * 2**20
        ),
    )(query_in, key_in, value_in, cotangent, filters, doc_lengths, w_out)
    shapes = [jax.ShapeDtypeStruct(r.shape, r.dtype) for r in results]
    hbm = pl.BlockSpec(memory_space=pl.ANY)
    big = len(results) - 1
    return tuple(
        pl.pallas_call(
            hand_over,
            in_specs=[hbm] * big + [vmem],
            out_specs=[hbm] * big + [vmem],
            out_shape=shapes,
            scratch_shapes=[pltpu.VMEM(r.shape, r.dtype) for r in shapes[:big]]
            + [dma((big,)), dma((big,))],
            compiler_params=pltpu.CompilerParams(vmem_limit_bytes=56 * 2**20),
        )(*results)
    )


def program(n_seq, n_chan, *arrays):
    rows, width = arrays[0].shape
    groups, length = arrays[3].shape
    block = arrays[5].shape[1] // n_seq
    aligned = block % LANES == 0 and width % block == 0 and width % (2 * LANES) == 0
    even = n_seq % 2 == 0 and n_chan % 2 == 0 and n_seq >= 4 and rows % (16 * n_chan) == 0
    if aligned and even and rows == length == LANES and LANES * groups % width == 0:
        return fused_body(n_seq, n_chan, *arrays)
    return body(n_seq, *arrays)


def solution(mesh):
    act = P("seq", "chan")
    return jax.shard_map(
        functools.partial(program, mesh.shape["seq"], mesh.shape["chan"]),
        mesh=mesh,
        in_specs=(act, act, act, P("chan", None), P(), P("chan", None), act),
        out_specs=(act, act, act, act, P("chan", "seq"), P("chan", "seq")),
        check_vma=False,
    )
```

```python
import functools

import jax
import jax.numpy as jnp
from jax import lax
from jax.experimental import pallas as pl
from jax.experimental.pallas import tpu as pltpu
from jax.sharding import PartitionSpec as P

F32 = jnp.float32
BF16 = jnp.bfloat16
LANES = 128


def doc_start(positions, starts):
    before = starts[None, :] <= positions[:, None]
    return jnp.max(jnp.where(before, starts[None, :], 0), axis=1)


def toeplitz(row, rows, shift=0):
    wide = jnp.broadcast_to(row, (rows, row.shape[-1]))
    return pltpu.roll(wide, shift, 1, stride=1, stride_axis=0)


def group_lanes(rows, per_group, index):
    lane = lax.broadcasted_iota(jnp.int32, (rows, LANES), 1)
    return (lane >= index * per_group) & (lane < (index + 1) * per_group)


def forward_kernel(per_group, q_ref, prev_ref, own_ref, taps_ref, mask_ref, filt_ref, gated_ref):
    rows, width = q_ref.shape
    mask = mask_ref[...].astype(F32)
    per_tile = LANES // per_group
    for tile in range(width // LANES):
        cols = slice(tile * LANES, (tile + 1) * LANES)
        ext = jnp.concatenate([prev_ref[:, cols], own_ref[:, cols]], axis=0)
        acc = jnp.zeros((rows, LANES), F32)
        for g in range(per_tile):
            row = tile * per_tile + g
            band = (toeplitz(taps_ref[row : row + 1, :], rows) * mask).astype(BF16)
            res = jnp.dot(band, ext, preferred_element_type=F32)
            acc = jnp.where(group_lanes(rows, per_group, g), res, acc)
        filt_ref[:, cols] = acc
        gated_ref[:, cols] = (q_ref[:, cols].astype(F32) * acc).astype(BF16)


def backward_kernel(
    per_group, k_ref, v_ref, prev_ref, own_ref, gate_ref, next_ref, grad_in_ref, filt_ref, taps_ref,
    fmask_ref, bmask_ref, gq_ref, gk_ref, gv_ref, sums_ref,
):
    rows, width = k_ref.shape
    bmask = bmask_ref[...].astype(F32)
    fmask = fmask_ref[...].astype(F32)
    per_tile = LANES // per_group
    r = lax.broadcasted_iota(jnp.int32, (rows, rows), 0)
    c = lax.broadcasted_iota(jnp.int32, (rows, rows), 1)
    flip = jnp.where(r + c == rows - 1, 1.0, 0.0).astype(BF16)
    gq_ref[...] = (grad_in_ref[...] * filt_ref[...]).astype(BF16)
    for tile in range(width // LANES):
        cols = slice(tile * LANES, (tile + 1) * LANES)
        gate = gate_ref[:, cols]
        gext = jnp.concatenate([gate, next_ref[:, cols]], axis=0)
        ext = jnp.concatenate([prev_ref[:, cols], own_ref[:, cols]], axis=0)
        turned = jnp.dot(flip, gate, preferred_element_type=F32)
        acc = jnp.zeros((rows, LANES), F32)
        for g in range(per_tile):
            row = tile * per_tile + g
            lanes = group_lanes(rows, per_group, g)
            band = (toeplitz(taps_ref[row : row + 1, :], rows) * bmask).astype(BF16)
            res = jnp.dot(band, gext, preferred_element_type=F32)
            acc = jnp.where(lanes, res, acc)
            mine = jnp.where(lanes, turned, 0.0).astype(BF16)
            pair = lax.dot_general(
                mine, ext, (((1,), (1,)), ((), ())), preferred_element_type=F32
            )
            pair = pltpu.roll(pair * fmask, 0, 1, stride=1, stride_axis=0)
            sums_ref[row : row + 1, :] = jnp.sum(pair, axis=0, keepdims=True)
        gk_ref[:, cols] = (acc * v_ref[:, cols].astype(F32)).astype(BF16)
        gv_ref[:, cols] = (acc * k_ref[:, cols].astype(F32)).astype(BF16)


def prepare(tok_rows, filters, doc_lengths):
    group_count, length = filters.shape
    span = 2 * tok_rows
    starts = jnp.cumsum(doc_lengths) - doc_lengths
    first_row = lax.axis_index("seq") * tok_rows
    wide = jnp.arange(span, dtype=jnp.int32)
    own_pos = first_row + wide[:tok_rows]
    fmask = ((first_row - tok_rows + wide)[None, :] >= doc_start(own_pos, starts)[:, None]).astype(BF16)
    bmask = (own_pos[:, None] >= doc_start(first_row + wide, starts)[None, :]).astype(BF16)
    taps = filters.astype(F32)
    none = jnp.zeros((group_count, span - length), F32)
    back_taps = jnp.concatenate([taps, none], axis=1)
    fore_taps = jnp.roll(jnp.flip(back_taps, 1), tok_rows + 1, axis=1)
    return fore_taps, back_taps, fmask, bmask


def body(n_seq, query_in, key_in, value_in, filters, doc_lengths, w_out, cotangent):
    tok_rows, chan_count = query_in.shape
    group_count, length = filters.shape
    per_group = chan_count // group_count
    step = 2 * LANES if chan_count % (2 * LANES) == 0 else LANES
    step_groups = step // per_group
    span = 2 * tok_rows

    full_cot = lax.all_gather(cotangent, "chan", axis=1, tiled=True)

    product_kv = (key_in.astype(F32) * value_in.astype(F32)).astype(BF16)
    up = [(i, i + 1) for i in range(n_seq - 1)]
    down = [(i + 1, i) for i in range(n_seq - 1)]
    prev_kv = lax.ppermute(product_kv, "seq", up)

    fore_taps, back_taps, fmask, bmask = prepare(tok_rows, filters, doc_lengths)
    tile = pl.BlockSpec((tok_rows, step), lambda i: (0, i))
    rowspec = pl.BlockSpec((step_groups, span), lambda i: (i, 0))
    whole = pl.BlockSpec((tok_rows, span), lambda i: (0, 0))
    blocks = chan_count // step
    filtered, gated = pl.pallas_call(
        functools.partial(forward_kernel, per_group),
        grid=(blocks,),
        in_specs=[tile, tile, tile, rowspec, whole],
        out_specs=[tile, tile],
        out_shape=[
            jax.ShapeDtypeStruct((tok_rows, chan_count), F32),
            jax.ShapeDtypeStruct((tok_rows, chan_count), BF16),
        ],
    )(query_in, prev_kv, product_kv, fore_taps, fmask)

    gated_all = lax.all_gather(gated, "seq", axis=0, tiled=True)

    grad_in = jnp.einsum("tn,cn->tc", full_cot, w_out, preferred_element_type=F32)
    grad_gate = (grad_in * query_in.astype(F32)).astype(BF16)
    next_gate = lax.ppermute(grad_gate, "seq", down)
    cot_cols = lax.all_to_all(full_cot, "seq", split_axis=1, concat_axis=0, tiled=True)

    partial_out = jnp.dot(gated, w_out, preferred_element_type=F32)
    block_out = lax.psum_scatter(
        partial_out.astype(BF16), "chan", scatter_dimension=1, tiled=True
    )

    grad_query, grad_key, grad_value, sums = pl.pallas_call(
        functools.partial(backward_kernel, per_group),
        grid=(blocks,),
        in_specs=[tile] * 8 + [rowspec, whole, whole],
        out_specs=[tile] * 3 + [rowspec],
        out_shape=[jax.ShapeDtypeStruct((tok_rows, chan_count), BF16)] * 3
        + [jax.ShapeDtypeStruct((group_count, span), F32)],
    )(
        key_in, value_in, prev_kv, product_kv, grad_gate, next_gate, grad_in, filtered,
        back_taps, jnp.flip(fmask, 0), bmask,
    )
    tap_part = jnp.flip(sums[:, span - length :], 1)
    tap_sum = lax.psum_scatter(
        tap_part.astype(BF16), "seq", scatter_dimension=1, tiled=True
    ).astype(F32)

    weight = lax.dot_general(
        gated_all, cot_cols, (((0,), (0,)), ((), ())), preferred_element_type=F32
    ).astype(BF16)
    return (block_out, grad_query, grad_key, grad_value, weight, tap_sum)


def mega_kernel(
    per_group, n_seq, n_chan, chunks, q_ref, k_ref, v_ref, cot_ref, taps_ref, len_ref, w_hbm,
    out_ref, gq_ref, gk_ref, gv_ref, gw_ref, tap_ref,
    w_ref, kv_ref, prev_ref, gate_ref, next_ref, filt_ref, gin_ref, gall_ref, cots_ref, cotc_ref,
    psend_ref, precv_ref, tsend_ref, trecv_ref, sums_ref, fore_ref, back_ref, fmask_ref, rmask_ref,
    bmask_ref, cott_ref, turned_ref, w_sem, rim_send, rim_recv, cot_send, cot_recv, pass_send, pass_recv, part_send, part_recv,
    a2a_send, a2a_recv, share_send, share_recv, tap_send, tap_recv, line_send, line_recv,
    pair_send, pair_recv,
):
    rows, width = q_ref.shape
    span = 2 * rows
    block = gw_ref.shape[1]
    per_chan = width // block
    half = rows // 2
    per_tile = LANES // per_group
    piece = width // chunks
    piece_tiles = piece // LANES
    s = lax.axis_index("seq")
    c = lax.axis_index("chan")
    hops = n_seq // 2
    z = s // 2
    pair = s + 1 - 2 * (s % 2)
    mate = c + 1 - 2 * (c % 2)
    core = c % 2

    def remote(src, dst, send, recv, seq, chan):
        return pltpu.make_async_remote_copy(
            src_ref=src, dst_ref=dst, send_sem=send, recv_sem=recv,
            device_id=(seq, chan), device_id_type=pl.DeviceIdType.MESH,
        )

    w_copy = pltpu.make_async_copy(w_hbm, w_ref, w_sem)
    w_copy.start()

    barrier = pltpu.get_barrier_semaphore()
    for o in range(1, n_seq):
        pl.semaphore_signal(
            barrier, inc=1, device_id=(lax.rem(s + o, n_seq), c),
            device_id_type=pl.DeviceIdType.MESH,
        )
    for o in range(1, n_chan):
        pl.semaphore_signal(
            barrier, inc=1, device_id=(s, lax.rem(c + o, n_chan)),
            device_id_type=pl.DeviceIdType.MESH,
        )
    kv_ref[...] = (k_ref[...].astype(F32) * v_ref[...].astype(F32)).astype(BF16)
    cots_ref[c] = cot_ref[...]

    row = lax.broadcasted_iota(jnp.int32, (rows, span), 0) + s * rows
    lane = lax.broadcasted_iota(jnp.int32, (rows, span), 1) + s * rows
    turned_row = 2 * s * rows + rows - 1 - row

    def first(pos):
        best = jnp.zeros_like(pos)
        start = jnp.int32(0)
        for d in range(len_ref.shape[0]):
            best = jnp.where(start <= pos, start, best)
            start = start + len_ref[d]
        return best

    fmask_ref[...] = jnp.where(lane - rows >= first(row), 1.0, 0.0)
    rmask_ref[...] = jnp.where(lane - rows >= first(turned_row), 1.0, 0.0)
    bmask_ref[...] = jnp.where(row >= first(lane), 1.0, 0.0)
    r = lax.broadcasted_iota(jnp.int32, (rows, rows), 0)
    cc = lax.broadcasted_iota(jnp.int32, (rows, rows), 1)
    turn = jnp.where(r + cc == rows - 1, 1.0, 0.0).astype(BF16)
    back_ref[...] = taps_ref[...].astype(F32)
    fore_ref[...] = jnp.dot(taps_ref[...], turn, preferred_element_type=F32)

    @pl.when(s == 0)
    def _():
        prev_ref[...] = jnp.zeros_like(prev_ref)

    @pl.when(s == n_seq - 1)
    def _():
        next_ref[...] = jnp.zeros_like(next_ref)

    pl.semaphore_wait(barrier, n_seq + n_chan - 2)

    def rim(index, src, dst, ch, to):
        cols = pl.ds(ch * piece, piece)
        return remote(
            src.at[:, cols], dst.at[:, cols], rim_send.at[index, ch], rim_recv.at[index, ch], to, c
        )

    @pl.when(s < n_seq - 1)
    def _():
        for ch in range(chunks):
            rim(0, kv_ref, prev_ref, ch, s + 1).start()

    def cot_copy(o):
        to = mate if o == 0 else lax.rem(c + 2 * o, n_chan)
        return remote(cot_ref, cots_ref.at[c], cot_send.at[o], cot_recv.at[o], s, to)

    def cot_pass(o):
        came = lax.rem(c + n_chan - 2 * o, n_chan)
        return remote(
            cots_ref.at[came], cots_ref.at[came], pass_send.at[o], pass_recv.at[o], s, mate
        )

    chips = n_chan // 2
    for o in range(1, chips):
        cot_copy(o).start()
    cot_copy(0).start()

    own_rows = pl.ds(pl.multiple_of(s * rows, rows), rows)

    def line(side, h, ch, seq):
        rows_of = pl.ds(pl.multiple_of(seq * rows, rows), rows)
        part = gall_ref.at[rows_of, pl.ds(ch * piece, piece)]
        to = s + 2 if side == 0 else s - 2
        return remote(part, part, line_send.at[side, h, ch], line_recv.at[side, h, ch], to, c)

    def across(side, h, ch, seq):
        rows_of = pl.ds(pl.multiple_of(seq * rows, rows), rows)
        part = gall_ref.at[rows_of, pl.ds(ch * piece, piece)]
        return remote(part, part, pair_send.at[side, h, ch], pair_recv.at[side, h, ch], pair, c)

    def pass_on(h, ch):
        up, down = s - 2 * h, s + 2 * h
        if h > 0:
            @pl.when(z - h >= 0)
            def _():
                line(0, h - 1, ch, up).wait_recv()

        @pl.when((z - h >= 0) & (z < hops - 1))
        def _():
            line(0, h, ch, up).start()

        @pl.when(z - h >= 0)
        def _():
            across(0, h, ch, up).start()

        if h > 0:
            @pl.when(z + h < hops)
            def _():
                line(1, h - 1, ch, down).wait_recv()

        @pl.when((z + h < hops) & (z > 0))
        def _():
            line(1, h, ch, down).start()

        if h > 0:
            @pl.when(z + h < hops)
            def _():
                across(1, h, ch, down).start()

    for ch in range(chunks):
        @pl.when(s > 0)
        def _():
            rim(0, kv_ref, prev_ref, ch, s).wait_recv()

        @pl.loop(ch * piece_tiles, (ch + 1) * piece_tiles)
        def _(tile):
            cols = pl.ds(pl.multiple_of(tile * LANES, LANES), LANES)
            mask = fmask_ref[...]
            taps = fore_ref[pl.ds(pl.multiple_of(tile * per_tile, per_tile), per_tile), :]
            taps = jnp.concatenate([taps, jnp.zeros_like(taps)], axis=1)
            ext = jnp.concatenate([prev_ref[:, cols], kv_ref[:, cols]], axis=0)
            acc = jnp.zeros((rows, LANES), F32)
            for g in range(per_tile):
                band = (toeplitz(taps[g : g + 1, :], rows, 1) * mask).astype(BF16)
                res = jnp.dot(band, ext, preferred_element_type=F32)
                acc = jnp.where(group_lanes(rows, per_group, g), res, acc)
            filt_ref[:, cols] = acc
            gall_ref[own_rows, cols] = (q_ref[:, cols].astype(F32) * acc).astype(BF16)

        pass_on(0, ch)

    for o in range(1, chips):
        cot_copy(o).wait_recv()
        cot_pass(o).start()
    cot_copy(0).wait_recv()
    w_copy.wait()
    for o in range(1, chips):
        cot_pass(o).wait_recv()

    def a2a_copy(o):
        to = lax.rem(s + o, n_seq)
        half_rows = pl.ds(pl.multiple_of(core * half, half), half)
        src = cots_ref.at[
            to // per_chan, half_rows, pl.ds(pl.multiple_of((to % per_chan) * block, block), block)
        ]
        dst = cotc_ref.at[pl.ds(pl.multiple_of(s * rows + core * half, half), half), :]
        return remote(src, dst, a2a_send.at[o], a2a_recv.at[o], to, c)

    for o in range(1, n_seq):
        a2a_copy(o).start()

    for p in range(n_chan):
        cott_ref[p * width : (p + 1) * width, :] = cots_ref[p].T

    in_tile = 2 * LANES
    piece_ins = piece // in_tile

    for ch in range(chunks):
        cols = pl.ds(ch * piece, piece)
        acc = jnp.dot(w_ref[cols, :], cott_ref[...], preferred_element_type=F32).T
        gin_ref[:, cols] = acc
        gate_ref[:, cols] = (acc * q_ref[:, cols].astype(F32)).astype(BF16)

        @pl.when(s > 0)
        def _():
            rim(1, gate_ref, next_ref, ch, s - 1).start()

        pass_on(1, ch)

    cotc_ref[own_rows, :] = cots_ref[
        s // per_chan, :, pl.ds(pl.multiple_of((s % per_chan) * block, block), block)
    ]

    def part_copy(o):
        to = lax.rem(c + o, n_chan)
        return remote(
            psend_ref.at[to], precv_ref.at[c], part_send.at[o], part_recv.at[o], s, to
        )

    gated = gall_ref.at[own_rows, :]
    later = [(h, ch) for h in range(2, hops) for ch in range(chunks)]
    waiting = later[:chunks]
    for o in range(1, n_chan + 1):
        to = lax.rem(c + o, n_chan)
        dest = psend_ref if o < n_chan else precv_ref

        @pl.loop(0, width // in_tile)
        def _(tile):
            cols = pl.ds(pl.multiple_of(tile * in_tile, in_tile), in_tile)
            w_cols = pl.ds(pl.multiple_of(to * width + tile * in_tile, in_tile), in_tile)
            dest[to, :, cols] = jnp.dot(
                gated[...], w_ref[:, w_cols], preferred_element_type=F32
            ).astype(BF16)

        if o < n_chan:
            part_copy(o).start()
        if waiting:
            pass_on(*waiting.pop(0))
    for left in waiting:
        pass_on(*left)

    def share_copy(o):
        came = lax.rem(s + n_seq - o, n_seq)
        at = pl.ds(pl.multiple_of(came * rows + core * half, half), half)
        return remote(
            cotc_ref.at[at, :], cotc_ref.at[at, :], share_send.at[o], share_recv.at[o], s, mate
        )

    waiting = later[chunks:]
    for ch in range(chunks):
        @pl.when(s < n_seq - 1)
        def _():
            rim(1, gate_ref, next_ref, ch, s).wait_recv()

        @pl.loop(ch * piece_tiles, (ch + 1) * piece_tiles)
        def _(tile):
            cols = pl.ds(pl.multiple_of(tile * LANES, LANES), LANES)
            at = pl.ds(pl.multiple_of(tile * per_tile, per_tile), per_tile)
            bmask = bmask_ref[...]
            rmask = rmask_ref[...]
            taps = back_ref[at, :]
            taps = jnp.concatenate([taps, jnp.zeros_like(taps)], axis=1)
            gate = gate_ref[:, cols]
            gext = jnp.concatenate([gate, next_ref[:, cols]], axis=0)
            ext = jnp.concatenate([prev_ref[:, cols], kv_ref[:, cols]], axis=0)
            turned = jnp.dot(turn, gate, preferred_element_type=F32)
            acc = jnp.zeros((rows, LANES), F32)
            found = []
            for g in range(per_tile):
                lanes = group_lanes(rows, per_group, g)
                band = (toeplitz(taps[g : g + 1, :], rows) * bmask).astype(BF16)
                res = jnp.dot(band, gext, preferred_element_type=F32)
                acc = jnp.where(lanes, res, acc)
                mine = jnp.where(lanes, turned, 0.0).astype(BF16)
                terms = lax.dot_general(
                    mine, ext, (((1,), (1,)), ((), ())), preferred_element_type=F32
                )
                terms = pltpu.roll(terms * rmask, 0, 1, stride=1, stride_axis=0)
                found.append(jnp.sum(terms, axis=0, keepdims=True))
            sums_ref[at, :] = jnp.concatenate(found, axis=0)
            gq_ref[:, cols] = (gin_ref[:, cols] * filt_ref[:, cols]).astype(BF16)
            gk_ref[:, cols] = (acc * v_ref[:, cols].astype(F32)).astype(BF16)
            gv_ref[:, cols] = (acc * k_ref[:, cols].astype(F32)).astype(BF16)

        if waiting:
            pass_on(*waiting.pop(0))
    for left in waiting:
        pass_on(*left)

    tsend_ref[...] = jnp.dot(
        sums_ref[:, span - LANES :].astype(BF16), turn, preferred_element_type=F32
    ).astype(BF16)

    def tap_copy(o):
        return remote(
            tsend_ref, trecv_ref.at[s], tap_send.at[o], tap_recv.at[o], lax.rem(s + o, n_seq), c
        )

    for o in range(1, n_seq):
        tap_copy(o).start()
    trecv_ref[s] = tsend_ref[...]

    for o in range(1, n_seq):
        a2a_copy(o).wait_recv()
        share_copy(o).start()

    for o in range(1, n_chan):
        part_copy(o).wait_recv()

    @pl.loop(0, width // in_tile)
    def _(tile):
        cols = pl.ds(pl.multiple_of(tile * in_tile, in_tile), in_tile)
        acc = precv_ref[0, :, cols].astype(F32)
        for p in range(1, n_chan):
            acc = acc + precv_ref[p, :, cols].astype(F32)
        out_ref[:, cols] = acc.astype(BF16)

    for o in range(1, n_seq):
        tap_copy(o).wait_recv()
    total = trecv_ref[0].astype(F32)
    for p in range(1, n_seq):
        total = total + trecv_ref[p].astype(F32)
    share = tap_ref.shape[0]
    turned_ref[...] = total.T
    tap_ref[...] = turned_ref[pl.ds(pl.multiple_of(s * share, share), share), :]

    for o in range(1, n_seq):
        share_copy(o).wait_recv()
    for ch in range(chunks):
        for h in range(hops):
            @pl.when(z - h >= 0)
            def _():
                across(0, h, ch, s - 2 * h).wait_recv()

            if h > 0:
                @pl.when(z + h < hops)
                def _():
                    across(1, h, ch, s + 2 * h).wait_recv()

        @pl.loop(ch * piece_ins, (ch + 1) * piece_ins)
        def _(tile):
            cols = pl.ds(pl.multiple_of(tile * in_tile, in_tile), in_tile)
            gw_ref[cols, :] = lax.dot_general(
                gall_ref[:, cols], cotc_ref[...], (((0,), (0,)), ((), ())),
                preferred_element_type=F32,
            ).astype(BF16)

    for ch in range(chunks):
        @pl.when(s < n_seq - 1)
        def _():
            rim(0, kv_ref, prev_ref, ch, s + 1).wait_send()

        @pl.when(s > 0)
        def _():
            rim(1, gate_ref, next_ref, ch, s - 1).wait_send()

    for o in range(chips):
        cot_copy(o).wait_send()
    for o in range(1, chips):
        cot_pass(o).wait_send()
    for o in range(1, n_chan):
        part_copy(o).wait_send()
    for o in range(1, n_seq):
        a2a_copy(o).wait_send()
        share_copy(o).wait_send()
        tap_copy(o).wait_send()
    for h in range(hops):
        for ch in range(chunks):
            @pl.when((z - h >= 0) & (z < hops - 1))
            def _():
                line(0, h, ch, s - 2 * h).wait_send()

            @pl.when((z + h < hops) & (z > 0))
            def _():
                line(1, h, ch, s + 2 * h).wait_send()

            @pl.when(z - h >= 0)
            def _():
                across(0, h, ch, s - 2 * h).wait_send()

            if h > 0:
                @pl.when(z + h < hops)
                def _():
                    across(1, h, ch, s + 2 * h).wait_send()


def hand_over(*refs):
    big = (len(refs) - 4) // 3
    ins, tap_in = refs[:big], refs[big]
    outs, tap_out = refs[big + 1 : 2 * big + 1], refs[2 * big + 1]
    held, in_sem, out_sem = refs[2 * big + 2 : 3 * big + 2], refs[-2], refs[-1]
    loads = [pltpu.make_async_copy(ins[i], held[i], in_sem.at[i]) for i in range(big)]
    stores = [pltpu.make_async_copy(held[i], outs[i], out_sem.at[i]) for i in range(big)]
    for load in loads:
        load.start()
    tap_out[...] = tap_in[...]
    for load, store in zip(loads, stores):
        load.wait()
        store.start()
    for store in stores:
        store.wait()


def fused_body(n_seq, n_chan, query_in, key_in, value_in, filters, doc_lengths, w_out, cotangent):
    rows, width = query_in.shape
    groups, length = filters.shape
    per_group = width // groups
    block = w_out.shape[1] // n_seq
    ins = width // (2 * LANES)
    chunks = 3 if ins % 3 == 0 else 2 if ins % 2 == 0 else 1
    vmem = pl.BlockSpec(memory_space=pltpu.VMEM)
    act = jax.ShapeDtypeStruct((rows, width), BF16)
    dma = pltpu.SemaphoreType.DMA
    hops = n_seq // 2
    results = pl.pallas_call(
        functools.partial(mega_kernel, per_group, n_seq, n_chan, chunks),
        in_specs=[vmem] * 5
        + [pl.BlockSpec(memory_space=pltpu.SMEM), pl.BlockSpec(memory_space=pl.ANY)],
        out_specs=[vmem] * 6,
        out_shape=[act] * 4
        + [
            jax.ShapeDtypeStruct((width, block), BF16),
            jax.ShapeDtypeStruct((length // n_seq, groups), F32),
        ],
        scratch_shapes=[
            pltpu.VMEM(w_out.shape, BF16),
            pltpu.VMEM((rows, width), BF16),
            pltpu.VMEM((rows, width), BF16),
            pltpu.VMEM((rows, width), BF16),
            pltpu.VMEM((rows, width), BF16),
            pltpu.VMEM((rows, width), F32),
            pltpu.VMEM((rows, width), F32),
            pltpu.VMEM((n_seq * rows, width), BF16),
            pltpu.VMEM((n_chan, rows, width), BF16),
            pltpu.VMEM((n_seq * rows, block), BF16),
            pltpu.VMEM((n_chan, rows, width), BF16),
            pltpu.VMEM((n_chan, rows, width), BF16),
            pltpu.VMEM((groups, length), BF16),
            pltpu.VMEM((n_seq, groups, length), BF16),
            pltpu.VMEM((groups, 2 * rows), F32),
            pltpu.VMEM((groups, length), F32),
            pltpu.VMEM((groups, length), F32),
            pltpu.VMEM((rows, 2 * rows), F32),
            pltpu.VMEM((rows, 2 * rows), F32),
            pltpu.VMEM((rows, 2 * rows), F32),
            pltpu.VMEM((w_out.shape[1], rows), BF16),
            pltpu.VMEM((length, groups), F32),
            dma, dma((2, chunks)), dma((2, chunks)), dma((n_chan,)), dma((n_chan,)),
            dma((n_chan,)), dma((n_chan,)), dma((n_chan,)), dma((n_chan,)), dma((n_seq,)),
            dma((n_seq,)), dma((n_seq,)), dma((n_seq,)), dma((n_seq,)), dma((n_seq,)),
            dma((2, hops, chunks)), dma((2, hops, chunks)), dma((2, hops, chunks)),
            dma((2, hops, chunks)),
        ],
        compiler_params=pltpu.CompilerParams(
            collective_id=0, has_side_effects=True, vmem_limit_bytes=56 * 2**20
        ),
    )(query_in, key_in, value_in, cotangent, filters, doc_lengths, w_out)
    shapes = [jax.ShapeDtypeStruct(r.shape, r.dtype) for r in results]
    hbm = pl.BlockSpec(memory_space=pl.ANY)
    big = len(results) - 1
    results = pl.pallas_call(
        hand_over,
        in_specs=[hbm] * big + [vmem],
        out_specs=[hbm] * big + [vmem],
        out_shape=shapes,
        scratch_shapes=[pltpu.VMEM(r.shape, r.dtype) for r in shapes[:big]]
        + [dma((big,)), dma((big,))],
        compiler_params=pltpu.CompilerParams(vmem_limit_bytes=56 * 2**20),
    )(*results)
    return tuple(results[:big]) + (results[big].T,)


def program(n_seq, n_chan, *arrays):
    rows, width = arrays[0].shape
    groups, length = arrays[3].shape
    block = arrays[5].shape[1] // n_seq
    aligned = block % LANES == 0 and width % block == 0 and width % (2 * LANES) == 0
    even = n_seq % 2 == 0 and n_chan % 2 == 0 and n_seq >= 4 and length % (8 * n_seq) == 0
    if aligned and even and rows == length == LANES and LANES * groups % width == 0:
        return fused_body(n_seq, n_chan, *arrays)
    return body(n_seq, *arrays)


def solution(mesh):
    act = P("seq", "chan")
    return jax.shard_map(
        functools.partial(program, mesh.shape["seq"], mesh.shape["chan"]),
        mesh=mesh,
        in_specs=(act, act, act, P("chan", None), P(), P("chan", None), act),
        out_specs=(act, act, act, act, P("chan", "seq"), P("chan", "seq")),
        check_vma=False,
    )
```

```python
import functools

import jax
import jax.numpy as jnp
from jax import lax
from jax.experimental import pallas as pl
from jax.experimental.pallas import tpu as pltpu
from jax.sharding import PartitionSpec as P

F32 = jnp.float32
BF16 = jnp.bfloat16
LANES = 128


def doc_start(positions, starts):
    before = starts[None, :] <= positions[:, None]
    return jnp.max(jnp.where(before, starts[None, :], 0), axis=1)


def toeplitz(row, rows, shift=0):
    wide = jnp.broadcast_to(row, (rows, row.shape[-1]))
    return pltpu.roll(wide, shift, 1, stride=1, stride_axis=0)


def group_lanes(rows, per_group, index):
    lane = lax.broadcasted_iota(jnp.int32, (rows, LANES), 1)
    return (lane >= index * per_group) & (lane < (index + 1) * per_group)


def forward_kernel(per_group, q_ref, prev_ref, own_ref, taps_ref, mask_ref, filt_ref, gated_ref):
    rows, width = q_ref.shape
    mask = mask_ref[...].astype(F32)
    per_tile = LANES // per_group
    for tile in range(width // LANES):
        cols = slice(tile * LANES, (tile + 1) * LANES)
        ext = jnp.concatenate([prev_ref[:, cols], own_ref[:, cols]], axis=0)
        acc = jnp.zeros((rows, LANES), F32)
        for g in range(per_tile):
            row = tile * per_tile + g
            band = (toeplitz(taps_ref[row : row + 1, :], rows) * mask).astype(BF16)
            res = jnp.dot(band, ext, preferred_element_type=F32)
            acc = jnp.where(group_lanes(rows, per_group, g), res, acc)
        filt_ref[:, cols] = acc
        gated_ref[:, cols] = (q_ref[:, cols].astype(F32) * acc).astype(BF16)


def backward_kernel(
    per_group, k_ref, v_ref, prev_ref, own_ref, gate_ref, next_ref, grad_in_ref, filt_ref, taps_ref,
    fmask_ref, bmask_ref, gq_ref, gk_ref, gv_ref, sums_ref,
):
    rows, width = k_ref.shape
    bmask = bmask_ref[...].astype(F32)
    fmask = fmask_ref[...].astype(F32)
    per_tile = LANES // per_group
    r = lax.broadcasted_iota(jnp.int32, (rows, rows), 0)
    c = lax.broadcasted_iota(jnp.int32, (rows, rows), 1)
    flip = jnp.where(r + c == rows - 1, 1.0, 0.0).astype(BF16)
    gq_ref[...] = (grad_in_ref[...] * filt_ref[...]).astype(BF16)
    for tile in range(width // LANES):
        cols = slice(tile * LANES, (tile + 1) * LANES)
        gate = gate_ref[:, cols]
        gext = jnp.concatenate([gate, next_ref[:, cols]], axis=0)
        ext = jnp.concatenate([prev_ref[:, cols], own_ref[:, cols]], axis=0)
        turned = jnp.dot(flip, gate, preferred_element_type=F32)
        acc = jnp.zeros((rows, LANES), F32)
        for g in range(per_tile):
            row = tile * per_tile + g
            lanes = group_lanes(rows, per_group, g)
            band = (toeplitz(taps_ref[row : row + 1, :], rows) * bmask).astype(BF16)
            res = jnp.dot(band, gext, preferred_element_type=F32)
            acc = jnp.where(lanes, res, acc)
            mine = jnp.where(lanes, turned, 0.0).astype(BF16)
            pair = lax.dot_general(
                mine, ext, (((1,), (1,)), ((), ())), preferred_element_type=F32
            )
            pair = pltpu.roll(pair * fmask, 0, 1, stride=1, stride_axis=0)
            sums_ref[row : row + 1, :] = jnp.sum(pair, axis=0, keepdims=True)
        gk_ref[:, cols] = (acc * v_ref[:, cols].astype(F32)).astype(BF16)
        gv_ref[:, cols] = (acc * k_ref[:, cols].astype(F32)).astype(BF16)


def prepare(tok_rows, filters, doc_lengths):
    group_count, length = filters.shape
    span = 2 * tok_rows
    starts = jnp.cumsum(doc_lengths) - doc_lengths
    first_row = lax.axis_index("seq") * tok_rows
    wide = jnp.arange(span, dtype=jnp.int32)
    own_pos = first_row + wide[:tok_rows]
    fmask = ((first_row - tok_rows + wide)[None, :] >= doc_start(own_pos, starts)[:, None]).astype(BF16)
    bmask = (own_pos[:, None] >= doc_start(first_row + wide, starts)[None, :]).astype(BF16)
    taps = filters.astype(F32)
    none = jnp.zeros((group_count, span - length), F32)
    back_taps = jnp.concatenate([taps, none], axis=1)
    fore_taps = jnp.roll(jnp.flip(back_taps, 1), tok_rows + 1, axis=1)
    return fore_taps, back_taps, fmask, bmask


def body(n_seq, query_in, key_in, value_in, filters, doc_lengths, w_out, cotangent):
    tok_rows, chan_count = query_in.shape
    group_count, length = filters.shape
    per_group = chan_count // group_count
    step = 2 * LANES if chan_count % (2 * LANES) == 0 else LANES
    step_groups = step // per_group
    span = 2 * tok_rows

    full_cot = lax.all_gather(cotangent, "chan", axis=1, tiled=True)

    product_kv = (key_in.astype(F32) * value_in.astype(F32)).astype(BF16)
    up = [(i, i + 1) for i in range(n_seq - 1)]
    down = [(i + 1, i) for i in range(n_seq - 1)]
    prev_kv = lax.ppermute(product_kv, "seq", up)

    fore_taps, back_taps, fmask, bmask = prepare(tok_rows, filters, doc_lengths)
    tile = pl.BlockSpec((tok_rows, step), lambda i: (0, i))
    rowspec = pl.BlockSpec((step_groups, span), lambda i: (i, 0))
    whole = pl.BlockSpec((tok_rows, span), lambda i: (0, 0))
    blocks = chan_count // step
    filtered, gated = pl.pallas_call(
        functools.partial(forward_kernel, per_group),
        grid=(blocks,),
        in_specs=[tile, tile, tile, rowspec, whole],
        out_specs=[tile, tile],
        out_shape=[
            jax.ShapeDtypeStruct((tok_rows, chan_count), F32),
            jax.ShapeDtypeStruct((tok_rows, chan_count), BF16),
        ],
    )(query_in, prev_kv, product_kv, fore_taps, fmask)

    gated_all = lax.all_gather(gated, "seq", axis=0, tiled=True)

    grad_in = jnp.einsum("tn,cn->tc", full_cot, w_out, preferred_element_type=F32)
    grad_gate = (grad_in * query_in.astype(F32)).astype(BF16)
    next_gate = lax.ppermute(grad_gate, "seq", down)
    cot_cols = lax.all_to_all(full_cot, "seq", split_axis=1, concat_axis=0, tiled=True)

    partial_out = jnp.dot(gated, w_out, preferred_element_type=F32)
    block_out = lax.psum_scatter(
        partial_out.astype(BF16), "chan", scatter_dimension=1, tiled=True
    )

    grad_query, grad_key, grad_value, sums = pl.pallas_call(
        functools.partial(backward_kernel, per_group),
        grid=(blocks,),
        in_specs=[tile] * 8 + [rowspec, whole, whole],
        out_specs=[tile] * 3 + [rowspec],
        out_shape=[jax.ShapeDtypeStruct((tok_rows, chan_count), BF16)] * 3
        + [jax.ShapeDtypeStruct((group_count, span), F32)],
    )(
        key_in, value_in, prev_kv, product_kv, grad_gate, next_gate, grad_in, filtered,
        back_taps, jnp.flip(fmask, 0), bmask,
    )
    tap_part = jnp.flip(sums[:, span - length :], 1)
    tap_sum = lax.psum_scatter(
        tap_part.astype(BF16), "seq", scatter_dimension=1, tiled=True
    ).astype(F32)

    weight = lax.dot_general(
        gated_all, cot_cols, (((0,), (0,)), ((), ())), preferred_element_type=F32
    ).astype(BF16)
    return (block_out, grad_query, grad_key, grad_value, weight, tap_sum)


def mega_kernel(
    per_group, n_seq, n_chan, chunks, q_ref, k_ref, v_ref, cot_ref, taps_ref, len_ref, w_hbm,
    out_ref, gq_ref, gk_ref, gv_ref, gw_ref, tap_ref,
    w_ref, kv_ref, prev_ref, gate_ref, next_ref, filt_ref, gin_ref, gall_ref, cots_ref, cotc_ref,
    psend_ref, precv_ref, tsend_ref, trecv_ref, sums_ref, fore_ref, back_ref, fmask_ref, rmask_ref,
    bmask_ref, cott_ref, turned_ref, w_sem, rim_send, rim_recv, cot_send, cot_recv, pass_send, pass_recv, part_send, part_recv,
    a2a_send, a2a_recv, share_send, share_recv, tap_send, tap_recv, line_send, line_recv,
    pair_send, pair_recv,
):
    rows, width = q_ref.shape
    span = 2 * rows
    block = gw_ref.shape[1]
    per_chan = width // block
    share_rows = rows // n_chan
    per_tile = LANES // per_group
    piece = width // chunks
    piece_tiles = piece // LANES
    s = lax.axis_index("seq")
    c = lax.axis_index("chan")
    hops = n_seq // 2
    z = s // 2
    pair = s + 1 - 2 * (s % 2)
    mate = c + 1 - 2 * (c % 2)

    def remote(src, dst, send, recv, seq, chan):
        return pltpu.make_async_remote_copy(
            src_ref=src, dst_ref=dst, send_sem=send, recv_sem=recv,
            device_id=(seq, chan), device_id_type=pl.DeviceIdType.MESH,
        )

    w_copy = pltpu.make_async_copy(w_hbm, w_ref, w_sem)
    w_copy.start()

    barrier = pltpu.get_barrier_semaphore()
    for o in range(1, n_seq):
        pl.semaphore_signal(
            barrier, inc=1, device_id=(lax.rem(s + o, n_seq), c),
            device_id_type=pl.DeviceIdType.MESH,
        )
    for o in range(1, n_chan):
        pl.semaphore_signal(
            barrier, inc=1, device_id=(s, lax.rem(c + o, n_chan)),
            device_id_type=pl.DeviceIdType.MESH,
        )
    kv_ref[...] = (k_ref[...].astype(F32) * v_ref[...].astype(F32)).astype(BF16)
    cots_ref[c] = cot_ref[...]

    row = lax.broadcasted_iota(jnp.int32, (rows, span), 0) + s * rows
    lane = lax.broadcasted_iota(jnp.int32, (rows, span), 1) + s * rows
    turned_row = 2 * s * rows + rows - 1 - row

    def first(pos):
        best = jnp.zeros_like(pos)
        start = jnp.int32(0)
        for d in range(len_ref.shape[0]):
            best = jnp.where(start <= pos, start, best)
            start = start + len_ref[d]
        return best

    fmask_ref[...] = jnp.where(lane - rows >= first(row), 1.0, 0.0)
    rmask_ref[...] = jnp.where(lane - rows >= first(turned_row), 1.0, 0.0)
    bmask_ref[...] = jnp.where(row >= first(lane), 1.0, 0.0)
    r = lax.broadcasted_iota(jnp.int32, (rows, rows), 0)
    cc = lax.broadcasted_iota(jnp.int32, (rows, rows), 1)
    turn = jnp.where(r + cc == rows - 1, 1.0, 0.0).astype(BF16)
    back_ref[...] = taps_ref[...].astype(F32)
    fore_ref[...] = jnp.dot(taps_ref[...], turn, preferred_element_type=F32)

    @pl.when(s == 0)
    def _():
        prev_ref[...] = jnp.zeros_like(prev_ref)

    @pl.when(s == n_seq - 1)
    def _():
        next_ref[...] = jnp.zeros_like(next_ref)

    pl.semaphore_wait(barrier, n_seq + n_chan - 2)

    def rim(index, src, dst, ch, to):
        cols = pl.ds(ch * piece, piece)
        return remote(
            src.at[:, cols], dst.at[:, cols], rim_send.at[index, ch], rim_recv.at[index, ch], to, c
        )

    @pl.when(s < n_seq - 1)
    def _():
        for ch in range(chunks):
            rim(0, kv_ref, prev_ref, ch, s + 1).start()

    def cot_copy(o):
        to = mate if o == 0 else lax.rem(c + 2 * o, n_chan)
        return remote(cot_ref, cots_ref.at[c], cot_send.at[o], cot_recv.at[o], s, to)

    def cot_pass(o):
        came = lax.rem(c + n_chan - 2 * o, n_chan)
        return remote(
            cots_ref.at[came], cots_ref.at[came], pass_send.at[o], pass_recv.at[o], s, mate
        )

    chips = n_chan // 2
    for o in range(1, chips):
        cot_copy(o).start()
    cot_copy(0).start()

    own_rows = pl.ds(pl.multiple_of(s * rows, rows), rows)

    def line(side, h, ch, seq):
        rows_of = pl.ds(pl.multiple_of(seq * rows, rows), rows)
        part = gall_ref.at[rows_of, pl.ds(ch * piece, piece)]
        to = s + 2 if side == 0 else s - 2
        return remote(part, part, line_send.at[side, h, ch], line_recv.at[side, h, ch], to, c)

    def across(side, h, ch, seq):
        rows_of = pl.ds(pl.multiple_of(seq * rows, rows), rows)
        part = gall_ref.at[rows_of, pl.ds(ch * piece, piece)]
        return remote(part, part, pair_send.at[side, h, ch], pair_recv.at[side, h, ch], pair, c)

    def pass_on(h, ch):
        up, down = s - 2 * h, s + 2 * h
        if h > 0:
            @pl.when(z - h >= 0)
            def _():
                line(0, h - 1, ch, up).wait_recv()

        @pl.when((z - h >= 0) & (z < hops - 1))
        def _():
            line(0, h, ch, up).start()

        @pl.when(z - h >= 0)
        def _():
            across(0, h, ch, up).start()

        if h > 0:
            @pl.when(z + h < hops)
            def _():
                line(1, h - 1, ch, down).wait_recv()

        @pl.when((z + h < hops) & (z > 0))
        def _():
            line(1, h, ch, down).start()

        if h > 0:
            @pl.when(z + h < hops)
            def _():
                across(1, h, ch, down).start()

    for ch in range(chunks):
        @pl.when(s > 0)
        def _():
            rim(0, kv_ref, prev_ref, ch, s).wait_recv()

        @pl.loop(ch * piece_tiles, (ch + 1) * piece_tiles)
        def _(tile):
            cols = pl.ds(pl.multiple_of(tile * LANES, LANES), LANES)
            mask = fmask_ref[...]
            taps = fore_ref[pl.ds(pl.multiple_of(tile * per_tile, per_tile), per_tile), :]
            taps = jnp.concatenate([taps, jnp.zeros_like(taps)], axis=1)
            ext = jnp.concatenate([prev_ref[:, cols], kv_ref[:, cols]], axis=0)
            acc = jnp.zeros((rows, LANES), F32)
            for g in range(per_tile):
                band = (toeplitz(taps[g : g + 1, :], rows, 1) * mask).astype(BF16)
                res = jnp.dot(band, ext, preferred_element_type=F32)
                acc = jnp.where(group_lanes(rows, per_group, g), res, acc)
            filt_ref[:, cols] = acc
            gall_ref[own_rows, cols] = (q_ref[:, cols].astype(F32) * acc).astype(BF16)

        pass_on(0, ch)

    for o in range(1, chips):
        cot_copy(o).wait_recv()
        cot_pass(o).start()
    cot_copy(0).wait_recv()
    w_copy.wait()
    for o in range(1, chips):
        cot_pass(o).wait_recv()

    def a2a_copy(o):
        to = lax.rem(s + o, n_seq)
        my_rows = pl.ds(pl.multiple_of(c * share_rows, share_rows), share_rows)
        src = cots_ref.at[
            to // per_chan, my_rows, pl.ds(pl.multiple_of((to % per_chan) * block, block), block)
        ]
        at = pl.multiple_of(s * rows + c * share_rows, share_rows)
        dst = cotc_ref.at[pl.ds(at, share_rows), :]
        return remote(src, dst, a2a_send.at[o], a2a_recv.at[o], to, c)

    for o in range(1, n_seq):
        a2a_copy(o).start()

    for p in range(n_chan):
        cott_ref[p * width : (p + 1) * width, :] = cots_ref[p].T

    in_tile = 2 * LANES
    piece_ins = piece // in_tile

    for ch in range(chunks):
        cols = pl.ds(ch * piece, piece)
        acc = jnp.dot(w_ref[cols, :], cott_ref[...], preferred_element_type=F32).T
        gin_ref[:, cols] = acc
        gate_ref[:, cols] = (acc * q_ref[:, cols].astype(F32)).astype(BF16)

        @pl.when(s > 0)
        def _():
            rim(1, gate_ref, next_ref, ch, s - 1).start()

        pass_on(1, ch)

    cotc_ref[own_rows, :] = cots_ref[
        s // per_chan, :, pl.ds(pl.multiple_of((s % per_chan) * block, block), block)
    ]

    def part_copy(o):
        to = lax.rem(c + o, n_chan)
        return remote(
            psend_ref.at[to], precv_ref.at[c], part_send.at[o], part_recv.at[o], s, to
        )

    gated = gall_ref.at[own_rows, :]
    later = [(h, ch) for h in range(2, hops) for ch in range(chunks)]
    waiting = later[:chunks]
    for o in range(1, n_chan + 1):
        to = lax.rem(c + o, n_chan)
        dest = psend_ref if o < n_chan else precv_ref

        @pl.loop(0, width // in_tile)
        def _(tile):
            cols = pl.ds(pl.multiple_of(tile * in_tile, in_tile), in_tile)
            w_cols = pl.ds(pl.multiple_of(to * width + tile * in_tile, in_tile), in_tile)
            dest[to, :, cols] = jnp.dot(
                gated[...], w_ref[:, w_cols], preferred_element_type=F32
            ).astype(BF16)

        if o < n_chan:
            part_copy(o).start()
        if waiting:
            pass_on(*waiting.pop(0))
    for left in waiting:
        pass_on(*left)

    def share_copy(o, peer):
        came = lax.rem(s + n_seq - o, n_seq)
        at = pl.multiple_of(came * rows + c * share_rows, share_rows)
        part = cotc_ref.at[pl.ds(at, share_rows), :]
        return remote(
            part, part, share_send.at[o, peer], share_recv.at[o, peer], s,
            lax.rem(c + peer, n_chan),
        )

    for o in range(1, n_seq):
        a2a_copy(o).wait_recv()
        for peer in range(1, n_chan):
            share_copy(o, peer).start()

    waiting = later[chunks:]
    for ch in range(chunks):
        @pl.when(s < n_seq - 1)
        def _():
            rim(1, gate_ref, next_ref, ch, s).wait_recv()

        @pl.loop(ch * piece_tiles, (ch + 1) * piece_tiles)
        def _(tile):
            cols = pl.ds(pl.multiple_of(tile * LANES, LANES), LANES)
            at = pl.ds(pl.multiple_of(tile * per_tile, per_tile), per_tile)
            bmask = bmask_ref[...]
            rmask = rmask_ref[...]
            taps = back_ref[at, :]
            taps = jnp.concatenate([taps, jnp.zeros_like(taps)], axis=1)
            gate = gate_ref[:, cols]
            gext = jnp.concatenate([gate, next_ref[:, cols]], axis=0)
            ext = jnp.concatenate([prev_ref[:, cols], kv_ref[:, cols]], axis=0)
            turned = jnp.dot(turn, gate, preferred_element_type=F32)
            acc = jnp.zeros((rows, LANES), F32)
            found = []
            for g in range(per_tile):
                lanes = group_lanes(rows, per_group, g)
                band = (toeplitz(taps[g : g + 1, :], rows) * bmask).astype(BF16)
                res = jnp.dot(band, gext, preferred_element_type=F32)
                acc = jnp.where(lanes, res, acc)
                mine = jnp.where(lanes, turned, 0.0).astype(BF16)
                terms = lax.dot_general(
                    mine, ext, (((1,), (1,)), ((), ())), preferred_element_type=F32
                )
                terms = pltpu.roll(terms * rmask, 0, 1, stride=1, stride_axis=0)
                found.append(jnp.sum(terms, axis=0, keepdims=True))
            sums_ref[at, :] = jnp.concatenate(found, axis=0)
            gq_ref[:, cols] = (gin_ref[:, cols] * filt_ref[:, cols]).astype(BF16)
            gk_ref[:, cols] = (acc * v_ref[:, cols].astype(F32)).astype(BF16)
            gv_ref[:, cols] = (acc * k_ref[:, cols].astype(F32)).astype(BF16)

        if waiting:
            pass_on(*waiting.pop(0))
    for left in waiting:
        pass_on(*left)

    tsend_ref[...] = jnp.dot(
        sums_ref[:, span - LANES :].astype(BF16), turn, preferred_element_type=F32
    ).astype(BF16)

    def tap_copy(o):
        return remote(
            tsend_ref, trecv_ref.at[s], tap_send.at[o], tap_recv.at[o], lax.rem(s + o, n_seq), c
        )

    for o in range(1, n_seq):
        tap_copy(o).start()
    trecv_ref[s] = tsend_ref[...]

    for o in range(1, n_chan):
        part_copy(o).wait_recv()

    @pl.loop(0, width // in_tile)
    def _(tile):
        cols = pl.ds(pl.multiple_of(tile * in_tile, in_tile), in_tile)
        acc = precv_ref[0, :, cols].astype(F32)
        for p in range(1, n_chan):
            acc = acc + precv_ref[p, :, cols].astype(F32)
        out_ref[:, cols] = acc.astype(BF16)

    for o in range(1, n_seq):
        tap_copy(o).wait_recv()
    total = trecv_ref[0].astype(F32)
    for p in range(1, n_seq):
        total = total + trecv_ref[p].astype(F32)
    share = tap_ref.shape[0]
    turned_ref[...] = total.T
    tap_ref[...] = turned_ref[pl.ds(pl.multiple_of(s * share, share), share), :]

    for o in range(1, n_seq):
        for peer in range(1, n_chan):
            share_copy(o, peer).wait_recv()
    for ch in range(chunks):
        for h in range(hops):
            @pl.when(z - h >= 0)
            def _():
                across(0, h, ch, s - 2 * h).wait_recv()

            if h > 0:
                @pl.when(z + h < hops)
                def _():
                    across(1, h, ch, s + 2 * h).wait_recv()

        @pl.loop(ch * piece_ins, (ch + 1) * piece_ins)
        def _(tile):
            cols = pl.ds(pl.multiple_of(tile * in_tile, in_tile), in_tile)
            gw_ref[cols, :] = lax.dot_general(
                gall_ref[:, cols], cotc_ref[...], (((0,), (0,)), ((), ())),
                preferred_element_type=F32,
            ).astype(BF16)

    for ch in range(chunks):
        @pl.when(s < n_seq - 1)
        def _():
            rim(0, kv_ref, prev_ref, ch, s + 1).wait_send()

        @pl.when(s > 0)
        def _():
            rim(1, gate_ref, next_ref, ch, s - 1).wait_send()

    for o in range(chips):
        cot_copy(o).wait_send()
    for o in range(1, chips):
        cot_pass(o).wait_send()
    for o in range(1, n_chan):
        part_copy(o).wait_send()
    for o in range(1, n_seq):
        a2a_copy(o).wait_send()
        for peer in range(1, n_chan):
            share_copy(o, peer).wait_send()
        tap_copy(o).wait_send()
    for h in range(hops):
        for ch in range(chunks):
            @pl.when((z - h >= 0) & (z < hops - 1))
            def _():
                line(0, h, ch, s - 2 * h).wait_send()

            @pl.when((z + h < hops) & (z > 0))
            def _():
                line(1, h, ch, s + 2 * h).wait_send()

            @pl.when(z - h >= 0)
            def _():
                across(0, h, ch, s - 2 * h).wait_send()

            if h > 0:
                @pl.when(z + h < hops)
                def _():
                    across(1, h, ch, s + 2 * h).wait_send()


def hand_over(*refs):
    big = (len(refs) - 4) // 3
    ins, tap_in = refs[:big], refs[big]
    outs, tap_out = refs[big + 1 : 2 * big + 1], refs[2 * big + 1]
    held, in_sem, out_sem = refs[2 * big + 2 : 3 * big + 2], refs[-2], refs[-1]
    loads = [pltpu.make_async_copy(ins[i], held[i], in_sem.at[i]) for i in range(big)]
    stores = [pltpu.make_async_copy(held[i], outs[i], out_sem.at[i]) for i in range(big)]
    for load in loads:
        load.start()
    tap_out[...] = tap_in[...]
    for load, store in zip(loads, stores):
        load.wait()
        store.start()
    for store in stores:
        store.wait()


def fused_body(n_seq, n_chan, query_in, key_in, value_in, filters, doc_lengths, w_out, cotangent):
    rows, width = query_in.shape
    groups, length = filters.shape
    per_group = width // groups
    block = w_out.shape[1] // n_seq
    ins = width // (2 * LANES)
    chunks = 3 if ins % 3 == 0 else 2 if ins % 2 == 0 else 1
    vmem = pl.BlockSpec(memory_space=pltpu.VMEM)
    act = jax.ShapeDtypeStruct((rows, width), BF16)
    dma = pltpu.SemaphoreType.DMA
    hops = n_seq // 2
    results = pl.pallas_call(
        functools.partial(mega_kernel, per_group, n_seq, n_chan, chunks),
        in_specs=[vmem] * 5
        + [pl.BlockSpec(memory_space=pltpu.SMEM), pl.BlockSpec(memory_space=pl.ANY)],
        out_specs=[vmem] * 6,
        out_shape=[act] * 4
        + [
            jax.ShapeDtypeStruct((width, block), BF16),
            jax.ShapeDtypeStruct((length // n_seq, groups), F32),
        ],
        scratch_shapes=[
            pltpu.VMEM(w_out.shape, BF16),
            pltpu.VMEM((rows, width), BF16),
            pltpu.VMEM((rows, width), BF16),
            pltpu.VMEM((rows, width), BF16),
            pltpu.VMEM((rows, width), BF16),
            pltpu.VMEM((rows, width), F32),
            pltpu.VMEM((rows, width), F32),
            pltpu.VMEM((n_seq * rows, width), BF16),
            pltpu.VMEM((n_chan, rows, width), BF16),
            pltpu.VMEM((n_seq * rows, block), BF16),
            pltpu.VMEM((n_chan, rows, width), BF16),
            pltpu.VMEM((n_chan, rows, width), BF16),
            pltpu.VMEM((groups, length), BF16),
            pltpu.VMEM((n_seq, groups, length), BF16),
            pltpu.VMEM((groups, 2 * rows), F32),
            pltpu.VMEM((groups, length), F32),
            pltpu.VMEM((groups, length), F32),
            pltpu.VMEM((rows, 2 * rows), F32),
            pltpu.VMEM((rows, 2 * rows), F32),
            pltpu.VMEM((rows, 2 * rows), F32),
            pltpu.VMEM((w_out.shape[1], rows), BF16),
            pltpu.VMEM((length, groups), F32),
            dma, dma((2, chunks)), dma((2, chunks)), dma((n_chan,)), dma((n_chan,)),
            dma((n_chan,)), dma((n_chan,)), dma((n_chan,)), dma((n_chan,)), dma((n_seq,)),
            dma((n_seq,)), dma((n_seq, n_chan)), dma((n_seq, n_chan)), dma((n_seq,)), dma((n_seq,)),
            dma((2, hops, chunks)), dma((2, hops, chunks)), dma((2, hops, chunks)),
            dma((2, hops, chunks)),
        ],
        compiler_params=pltpu.CompilerParams(
            collective_id=0, has_side_effects=True, vmem_limit_bytes=56 * 2**20
        ),
    )(query_in, key_in, value_in, cotangent, filters, doc_lengths, w_out)
    shapes = [jax.ShapeDtypeStruct(r.shape, r.dtype) for r in results]
    hbm = pl.BlockSpec(memory_space=pl.ANY)
    big = len(results) - 1
    results = pl.pallas_call(
        hand_over,
        in_specs=[hbm] * big + [vmem],
        out_specs=[hbm] * big + [vmem],
        out_shape=shapes,
        scratch_shapes=[pltpu.VMEM(r.shape, r.dtype) for r in shapes[:big]]
        + [dma((big,)), dma((big,))],
        compiler_params=pltpu.CompilerParams(vmem_limit_bytes=56 * 2**20),
    )(*results)
    return tuple(results[:big]) + (results[big].T,)


def program(n_seq, n_chan, *arrays):
    rows, width = arrays[0].shape
    groups, length = arrays[3].shape
    block = arrays[5].shape[1] // n_seq
    aligned = block % LANES == 0 and width % block == 0 and width % (2 * LANES) == 0
    even = n_seq % 2 == 0 and n_chan % 2 == 0 and n_seq >= 4 and rows % (16 * n_chan) == 0 and length % (8 * n_seq) == 0
    if aligned and even and rows == length == LANES and LANES * groups % width == 0:
        return fused_body(n_seq, n_chan, *arrays)
    return body(n_seq, *arrays)


def solution(mesh):
    act = P("seq", "chan")
    return jax.shard_map(
        functools.partial(program, mesh.shape["seq"], mesh.shape["chan"]),
        mesh=mesh,
        in_specs=(act, act, act, P("chan", None), P(), P("chan", None), act),
        out_specs=(act, act, act, act, P("chan", "seq"), P("chan", "seq")),
        check_vma=False,
    )
```
